128 devices in a mesh: prefix: 8 (over z, x_hi), group: 8 (over y, core), tensor: 2 (over x_lo).
Axes of the slice: x: 4 (x_hi: 2, x_lo: 2; x = x_hi * 2 + x_lo), y: 4, z: 4, core: 2. Of those that a mesh axis runs over, the one named last changes fastest.
Arguments:
- resp_query: bfloat16 [1024, 16, 32, 128], P('prefix', 'group', 'tensor'), may hold values from -6 to 6
- response_key: bfloat16 [1024, 16, 4, 128], P('prefix', 'group', 'tensor'), may hold values from -6 to 6
- response_value: bfloat16 [1024, 16, 4, 128], P('prefix', 'group', 'tensor'), may hold values from -6 to 6
- resp_cotangent: bfloat16 [1024, 16, 32, 128], P('prefix', 'group', 'tensor'), may hold values from -300 to 300
- prompt_key: bfloat16 [512, 4, 128], P('prefix', 'tensor'), may hold values from -6.2 to 6.2
- prompt_value_rows: bfloat16 [512, 4, 128], P('prefix', 'tensor'), may hold values from -6 to 6
- key_matrix: bfloat16 [5120, 512], P(None, 'tensor'), may hold values from -0.078125 to 0.078125
- value_matrix: bfloat16 [5120, 512], P(None, 'tensor'), may hold values from -0.078125 to 0.078125
- resp_lengths: int32 [16], replicated, may hold values from 256 to 1024, as said below
Outputs:
- resp_query_grad: bfloat16 [1024, 16, 32, 128], P('prefix', 'group', 'tensor')
- resp_key_grad: bfloat16 [1024, 16, 4, 128], P('prefix', 'group', 'tensor')
- resp_value_grad: bfloat16 [1024, 16, 4, 128], P('prefix', 'group', 'tensor')
- prompt_input_grad: bfloat16 [512, 5120], P('prefix', 'tensor')
The draws below stay inside these ranges and needn't reach their ends.
Inputs may be any that keep to these rules, and one draw needn't show every extreme that they name: `resp_lengths`: some response has all 1024 tokens and another 1024 // 4 in every draw.
All inputs are finite; a program needn't handle non-finite values.
Results may differ from the reference program's by a relative error of at most 0.0058.
Values may be sent and summed in bfloat16 or wider, within the bound.
No kernel may reach another device: no remote copies, remote signals or barrier semaphores. Data moves between devices by JAX's collectives and lax.ppermute only.
A program may use at most 128 MiB of HBM per device.

```python
import math
import jax
import jax.numpy as jnp
from jax import lax

MODEL_WIDTH = 5120
HEAD_SIZE = 128
QUERY_HEAD_COUNT = 32
KEY_VALUE_HEADS = 4
PROMPT_LENGTH = 512
RESPONSE_LENGTH = 1024
RESPONSE_COUNT = 16


def draw_resp_query(key, part):
    key = jax.random.fold_in(key, 11)
    key_first = jax.random.fold_in(key, 0)
    value_rows = jnp.clip(jax.random.normal(key_first, (RESPONSE_LENGTH, RESPONSE_COUNT, QUERY_HEAD_COUNT, HEAD_SIZE), jnp.float32), -6.0, 6.0)
    return value_rows.astype(jnp.bfloat16)


def draw_prompt_key(key, part):
    key = jax.random.fold_in(key, 23)
    key_first = jax.random.fold_in(key, 0)
    value_rows = jnp.clip(jax.random.normal(key_first, (PROMPT_LENGTH, KEY_VALUE_HEADS, HEAD_SIZE), jnp.float32), -6.0, 6.0)
    return value_rows.astype(jnp.bfloat16)


def draw_resp_lengths(key, part):
    key = jax.random.fold_in(key, 37)
    key_first, key_two, key_three = jax.random.split(key, 3)
    lengths = jax.random.randint(key_first, (RESPONSE_COUNT,), RESPONSE_LENGTH // 4, RESPONSE_LENGTH + 1)
    full_index = jax.random.randint(key_two, (), 0, RESPONSE_COUNT)
    short_index = (full_index + 1 + jax.random.randint(key_three, (), 0, RESPONSE_COUNT - 1)) % RESPONSE_COUNT
    row_ids = jnp.arange(RESPONSE_COUNT)
    lengths = jnp.where(row_ids == full_index, RESPONSE_LENGTH, lengths)
    lengths = jnp.where(row_ids == short_index, RESPONSE_LENGTH // 4, lengths)
    return lengths.astype(jnp.int32)


def shard_levels(stream_key, shape, shards, low, largest):
    gain, own = 1.0, jax.random.fold_in(stream_key, 6)
    for dim, shards_of in shards:
        draws = jnp.exp(jax.random.uniform(jax.random.fold_in(own, dim), (shards_of,), jnp.float32, low / len(shards), largest / len(shards)))
        gain = gain * jnp.repeat(draws, shape[dim] // shards_of).reshape([-1 if axis == dim else 1 for axis in range(len(shape))])
    return gain


def bell_draw(rng, dims, deviation, limit, cuts=(), kind=jnp.bfloat16):
    entries = deviation * jax.random.normal(rng, dims, jnp.float32)
    if cuts:
        entries = entries * shard_levels(rng, dims, cuts, -0.22, 0.18)
    return jnp.clip(entries, -limit, limit).astype(kind)


def setup_inputs(seed: int = 0) -> dict:
    seeds = jax.random.split(jax.random.key(seed), 10)
    resp_query = draw_resp_query(jax.random.fold_in(seeds[9], 71), 0)
    response_key = bell_draw(seeds[1], (RESPONSE_LENGTH, RESPONSE_COUNT, KEY_VALUE_HEADS, HEAD_SIZE), 1.0, 6.0, ((0, 8), (1, 8), (2, 2)))
    response_value = bell_draw(seeds[2], (RESPONSE_LENGTH, RESPONSE_COUNT, KEY_VALUE_HEADS, HEAD_SIZE), 1.0, 6.0, ((0, 8), (1, 8), (2, 2)))
    resp_cotangent = bell_draw(seeds[3], (RESPONSE_LENGTH, RESPONSE_COUNT, QUERY_HEAD_COUNT, HEAD_SIZE), 50.0, 300.0, ((0, 8), (1, 8), (2, 2)))
    prompt_key = draw_prompt_key(jax.random.fold_in(seeds[9], 71), 0)
    prompt_value_rows = bell_draw(seeds[5], (PROMPT_LENGTH, KEY_VALUE_HEADS, HEAD_SIZE), 1.0, 6.0, ((0, 8), (1, 2)))
    key_matrix = bell_draw(seeds[6], (MODEL_WIDTH, KEY_VALUE_HEADS * HEAD_SIZE), MODEL_WIDTH ** -0.5, 0.078125, ((1, 2),))
    value_matrix = bell_draw(seeds[7], (MODEL_WIDTH, KEY_VALUE_HEADS * HEAD_SIZE), MODEL_WIDTH ** -0.5, 0.078125, ((1, 2),))
    resp_lengths = draw_resp_lengths(jax.random.fold_in(seeds[9], 71), 0)
    return dict(resp_query=resp_query, response_key=response_key, response_value=response_value, resp_cotangent=resp_cotangent, prompt_key=prompt_key, prompt_value_rows=prompt_value_rows, key_matrix=key_matrix, value_matrix=value_matrix, resp_lengths=resp_lengths)


masked_score = -1e+30

def reference(resp_query, response_key, response_value, resp_cotangent, prompt_key, prompt_value_rows, key_matrix, value_matrix, resp_lengths):
    group_factor = QUERY_HEAD_COUNT // KEY_VALUE_HEADS
    score_scale = 1.0 / math.sqrt(HEAD_SIZE)
    prompt_keys = prompt_key.astype(jnp.float32)
    prompt_values = prompt_value_rows.astype(jnp.float32)
    positions = jnp.arange(RESPONSE_LENGTH, dtype=jnp.int32)
    key_pos = jnp.arange(PROMPT_LENGTH + RESPONSE_LENGTH, dtype=jnp.int32) - PROMPT_LENGTH
    visible = key_pos[None, :] <= positions[:, None]

    def one_response(state, pieces):
        query_first, key_first, value_one, cot_one, length_one = pieces
        query_float = query_first.reshape(RESPONSE_LENGTH, KEY_VALUE_HEADS, group_factor, HEAD_SIZE).astype(jnp.float32)
        live_rows = positions < length_one
        cotangent_active = jnp.where(live_rows[:, None, None], cot_one, jnp.zeros_like(cot_one))
        cotangent_float = cotangent_active.reshape(RESPONSE_LENGTH, KEY_VALUE_HEADS, group_factor, HEAD_SIZE).astype(jnp.float32)
        keys_f = jnp.concatenate([prompt_keys, key_first.astype(jnp.float32)], axis=0)
        values_f = jnp.concatenate([prompt_values, value_one.astype(jnp.float32)], axis=0)
        scores = jnp.einsum('lkge,mke->kglm', query_float, keys_f) * score_scale
        scores = jnp.where(visible, scores, masked_score)
        row_max = lax.optimization_barrier(jnp.max(scores, axis=-1))
        log_total = row_max + jnp.log(lax.optimization_barrier(jnp.sum(jnp.exp(scores - row_max[..., None]), axis=-1)))
        probs = jnp.exp(scores - log_total[..., None])
        dprob = jnp.einsum('lkge,mke->kglm', cotangent_float, values_f)
        row_delta = lax.optimization_barrier(jnp.sum(probs * dprob, axis=-1))
        dscore_low = lax.optimization_barrier((probs * (dprob - row_delta[..., None])).astype(jnp.bfloat16))
        prob_low = lax.optimization_barrier(probs.astype(jnp.bfloat16))
        dscore_f = dscore_low.astype(jnp.float32)
        prob_f = prob_low.astype(jnp.float32)
        value_sum = jnp.einsum('kglm,lkge->mke', prob_f, cotangent_float)
        key_sum = jnp.einsum('kglm,lkge->mke', dscore_f, query_float) * score_scale
        query_grad = jnp.einsum('kglm,mke->lkge', dscore_f, keys_f) * score_scale
        state = (state[0] + key_sum[:PROMPT_LENGTH], state[1] + value_sum[:PROMPT_LENGTH])
        outputs = (query_grad.reshape(RESPONSE_LENGTH, QUERY_HEAD_COUNT, HEAD_SIZE).astype(jnp.bfloat16), key_sum[PROMPT_LENGTH:].astype(jnp.bfloat16), value_sum[PROMPT_LENGTH:].astype(jnp.bfloat16))
        return (state, outputs)
    initial_state = (jnp.zeros((PROMPT_LENGTH, KEY_VALUE_HEADS, HEAD_SIZE), jnp.float32), jnp.zeros((PROMPT_LENGTH, KEY_VALUE_HEADS, HEAD_SIZE), jnp.float32))
    pieces = (jnp.moveaxis(resp_query, 1, 0), jnp.moveaxis(response_key, 1, 0), jnp.moveaxis(response_value, 1, 0), jnp.moveaxis(resp_cotangent, 1, 0), resp_lengths)
    prompt_totals, outputs = lax.scan(one_response, initial_state, pieces)
    prompt_key_gradient = prompt_totals[0].astype(jnp.bfloat16).reshape(PROMPT_LENGTH, KEY_VALUE_HEADS * HEAD_SIZE)
    prompt_value_gradient = prompt_totals[1].astype(jnp.bfloat16).reshape(PROMPT_LENGTH, KEY_VALUE_HEADS * HEAD_SIZE)
    prompt_input_grad = (jnp.dot(prompt_key_gradient, key_matrix.T, preferred_element_type=jnp.float32) + jnp.dot(prompt_value_gradient, value_matrix.T, preferred_element_type=jnp.float32)).astype(jnp.bfloat16)
    resp_query_grad = jnp.moveaxis(outputs[0], 0, 1)
    resp_key_grad = jnp.moveaxis(outputs[1], 0, 1)
    resp_value_grad = jnp.moveaxis(outputs[2], 0, 1)
    return (resp_query_grad, resp_key_grad, resp_value_grad, prompt_input_grad)
```

```python
import functools
import math

import jax
import jax.numpy as jnp
from jax import lax
from jax.experimental import pallas as pl
from jax.experimental.pallas import tpu as pltpu
from jax.sharding import PartitionSpec as P

MASKED = -1e30
F32 = jnp.float32
BF16 = jnp.bfloat16


def dot_nt(a, b):
    return lax.dot_general(a, b, (((1,), (1,)), ((), ())), preferred_element_type=F32)


def dot_nn(a, b):
    return lax.dot_general(a, b, (((1,), (0,)), ((), ())), preferred_element_type=F32)


def dot_tn(a, b):
    return lax.dot_general(a, b, (((0,), (0,)), ((), ())), preferred_element_type=F32)


def attention_kernel(tokens, zs, last, meta, q_ref, do_ref, pkv_ref, *refs):
    refs = list(refs)
    kv_refs = [refs.pop(0) for _ in range(zs)]
    prev_ref = refs.pop(0) if last else None
    dq_ref = refs.pop(0)
    dkv_refs = [refs.pop(0) for _ in range(zs)]
    dpkv_ref = refs.pop(0)
    e_ref, dp_ref, m_ref, l_ref, a_ref, mc_ref, dqt_ref = refs
    width = q_ref.shape[-1]
    rows = q_ref.shape[-2]
    scale = 1.0 / math.sqrt(width)
    log2 = scale * math.log2(math.e)
    z, xh, live = meta[0], meta[1], meta[2]
    prows = pkv_ref.shape[4]
    pchunks = pkv_ref.shape[0] // 2
    prompt_chunk = 4 * prows
    chunk = 2 * tokens
    prompt_rows = pchunks * prompt_chunk

    def prompt_pair(c, which):
        return pkv_ref[2 * c : 2 * c + 2, :, 0, which].reshape(prompt_chunk, width)

    def resp_pair(s, which):
        return kv_refs[s][:, 0, which].reshape(chunk, width)

    def forward(keys, values, base, index, mask):
        n = keys.shape[0]
        scores = dot_nt(keys, q_ref[0, 0])
        if mask is not None:
            scores = jnp.where(mask, scores, MASKED)
        top = jnp.max(scores, axis=0, keepdims=True)
        if index > 0:
            old = m_ref[...]
            top = jnp.maximum(old, top)
        e = jnp.exp2((scores - top) * log2)
        dp = dot_nt(values, do_ref[0, 0])
        esum = jnp.sum(e, axis=0, keepdims=True)
        dsum = jnp.sum(e * dp, axis=0, keepdims=True)
        if index > 0:
            fix = jnp.exp2((old - top) * log2)
            esum = esum + l_ref[...] * fix
            dsum = dsum + a_ref[...] * fix
        m_ref[...] = top
        l_ref[...] = esum
        a_ref[...] = dsum
        mc_ref[index] = top
        e_ref[base : base + n] = e
        dp_ref[base : base + n] = dp

    def backward(keys, base, index):
        n = keys.shape[0]
        inv = 1.0 / l_ref[...]
        factor = jnp.exp2((mc_ref[index] - m_ref[...]) * log2) * inv
        delta = a_ref[...] * inv
        p = e_ref[base : base + n] * factor
        ds = (p * (dp_ref[base : base + n] - delta)).astype(BF16)
        dv = dot_nn(p.astype(BF16), do_ref[0, 0])
        dk = dot_nn(ds, q_ref[0, 0]) * scale
        dqt = dot_tn(keys, ds)
        if index == 0:
            dqt_ref[...] = dqt
        else:
            dqt_ref[...] += dqt
        return dk, dv

    @pl.when(live > 0)
    def _():
        for c in range(pchunks):
            forward(prompt_pair(c, 0), prompt_pair(c, 1), c * prompt_chunk, c, None)
        for s in range(zs):
            def step(s=s):
                mask = None
                if s == 0:
                    row = lax.broadcasted_iota(jnp.int32, (chunk, rows), 0)
                    lane = lax.broadcasted_iota(jnp.int32, (chunk, rows), 1)
                    token = lax.rem(lane, tokens)
                    own = jnp.logical_and(row < tokens, row <= token)
                    other = jnp.logical_and(row >= tokens, xh > 0)
                    mask = jnp.logical_or(own, other)
                forward(resp_pair(s, 0), resp_pair(s, 1), prompt_rows + s * chunk, pchunks + s, mask)
            if s == 0:
                step()
            else:
                pl.when(z >= s)(step)
        for c in range(pchunks):
            dk, dv = backward(prompt_pair(c, 0), c * prompt_chunk, c)
            for which, term in ((0, dk), (1, dv)):
                term = term.reshape(2, 2, prows, width)
                if last:
                    term = term + prev_ref[2 * c : 2 * c + 2, :, 0, which]
                dpkv_ref[2 * c : 2 * c + 2, :, 0, which] = term.astype(dpkv_ref.dtype)
        for s in range(zs):
            def step(s=s):
                dk, dv = backward(resp_pair(s, 0), prompt_rows + s * chunk, pchunks + s)
                dkv_refs[s][:, 0, 0] = dk.reshape(2, tokens, width).astype(BF16)
                dkv_refs[s][:, 0, 1] = dv.reshape(2, tokens, width).astype(BF16)
            if s == 0:
                step()
            else:
                pl.when(z >= s)(step)
        dq_ref[0] = (dqt_ref[...] * scale).T.astype(BF16)

    @pl.when(live <= 0)
    def _():
        dq_ref[...] = jnp.zeros_like(dq_ref)
        for s in range(zs):
            dkv_refs[s][...] = jnp.zeros_like(dkv_refs[s])
        if last:
            dpkv_ref[...] = prev_ref[...].astype(dpkv_ref.dtype)
        else:
            dpkv_ref[...] = jnp.zeros_like(dpkv_ref)


def attention(meta, q, do, pkv, kvs, prev, r, tokens):
    zs = len(kvs)
    last = prev is not None
    kv_heads, rows, width = q.shape[1:]
    prows = pkv.shape[4]
    total = pkv.shape[0] * 2 * prows + zs * 2 * tokens
    qspec = pl.BlockSpec((1, 1, rows, width), lambda k, m: (r, k, 0, 0))
    pspec = pl.BlockSpec((pkv.shape[0], 2, 1, 2, prows, width), lambda k, m: (0, 0, k, 0, 0, 0))
    kspec = pl.BlockSpec((2, 1, 2, tokens, width), lambda k, m: (0, k, 0, 0, 0))
    in_specs = [qspec, qspec, pspec] + [kspec] * zs + ([pspec] if last else [])
    out_specs = [pl.BlockSpec((1, rows, width), lambda k, m: (k, 0, 0))] + [kspec] * zs + [pspec]
    out_shape = (
        [jax.ShapeDtypeStruct((kv_heads, rows, width), BF16)]
        + [jax.ShapeDtypeStruct(kvs[0].shape, BF16)] * zs
        + [jax.ShapeDtypeStruct(pkv.shape, BF16 if last else F32)]
    )
    slots = pkv.shape[0] // 2 + zs
    scratch = [
        pltpu.VMEM((total, rows), F32),
        pltpu.VMEM((total, rows), F32),
        pltpu.VMEM((1, rows), F32),
        pltpu.VMEM((1, rows), F32),
        pltpu.VMEM((1, rows), F32),
        pltpu.VMEM((slots, 1, rows), F32),
        pltpu.VMEM((width, rows), F32),
    ]
    args = [q, do, pkv] + list(kvs) + ([prev] if last else [])

    return pl.pallas_call(
        functools.partial(attention_kernel, tokens, zs, last),
        out_shape=out_shape,
        grid_spec=pltpu.PrefetchScalarGridSpec(
            num_scalar_prefetch=1,
            grid=(kv_heads,),
            in_specs=in_specs,
            out_specs=out_specs,
            scratch_shapes=scratch,
        ),
        compiler_params=pltpu.CompilerParams(vmem_limit_bytes=48 * 1024 * 1024),
        cost_estimate=pl.CostEstimate(
            flops=10 * kv_heads * rows * total * width,
            bytes_accessed=4 * 1024 * 1024,
            transcendentals=kv_heads * rows * total,
        ),
        name="attention_grad",
    )(meta, *args)


def per_device(
    resp_query,
    response_key,
    response_value,
    resp_cotangent,
    prompt_key,
    prompt_value_rows,
    key_matrix,
    value_matrix,
    resp_lengths,
):
    tokens, resp_count, query_heads, width = resp_query.shape
    kv_heads = response_key.shape[2]
    factor = query_heads // kv_heads
    prows = prompt_key.shape[0]
    prefix_size = lax.axis_size("prefix")
    group_size = lax.axis_size("group")
    zs = prefix_size // 2
    prefix = lax.axis_index("prefix")
    z, xh = prefix // 2, prefix % 2

    def swap(x):
        return lax.ppermute(x, "prefix", [(i, i ^ 1) for i in range(prefix_size)])

    def shift(x, s, wrap):
        pairs = [(i, i + 2 * s) for i in range(prefix_size)]
        if wrap:
            pairs = [(i, j % prefix_size) for i, j in pairs]
        else:
            pairs = [(i, j) for i, j in pairs if 0 <= j < prefix_size]
        return lax.ppermute(x, "prefix", pairs)

    prompt = jnp.stack((prompt_key, prompt_value_rows), 0).transpose(2, 0, 1, 3)
    resp = jnp.stack((response_key, response_value), 0).transpose(2, 3, 0, 1, 4)
    prompt_pair = jnp.stack((prompt, swap(prompt)))
    pkv = jnp.stack([prompt_pair] + [shift(prompt_pair, s, True) for s in range(1, zs)])
    kvs = []
    for r in range(resp_count):
        pair = jnp.stack((resp[r], swap(resp[r])))
        kvs.append([pair] + [shift(pair, s, False) for s in range(1, zs)])

    position = prefix * tokens + jnp.arange(tokens, dtype=jnp.int32)
    own_lengths = lax.dynamic_slice_in_dim(
        resp_lengths, lax.axis_index("group") * resp_count, resp_count
    )
    live_rows = position[:, None] < own_lengths[None, :]
    cot = jnp.where(live_rows[:, :, None, None], resp_cotangent, jnp.zeros_like(resp_cotangent))

    def to_rows(x):
        x = x.reshape(tokens, resp_count, kv_heads, factor, width)
        return x.transpose(1, 2, 3, 0, 4).reshape(resp_count, kv_heads, factor * tokens, width)

    q = to_rows(resp_query)
    do = to_rows(cot)
    live = (own_lengths > prefix * tokens).astype(jnp.int32)

    dqs, key_outs, value_outs = [], [], []
    dprompt = None
    for r in range(resp_count):
        meta = jnp.stack((z, xh, live[r])).astype(jnp.int32)
        outs = attention(meta, q, do, pkv, kvs[r], dprompt, r, tokens)
        dqs.append(outs[0])
        dkv = outs[1 : 1 + zs]
        dprompt = outs[1 + zs]
        total = dkv[0].astype(F32)
        for s in range(1, zs):
            total = total + shift(dkv[s], -s, False).astype(F32)
        total = total[0] + swap(total[1].astype(BF16)).astype(F32)
        total = total.astype(BF16)
        key_outs.append(total[:, 0])
        value_outs.append(total[:, 1])

    def from_rows(x):
        x = jnp.stack(x).reshape(resp_count, kv_heads, factor, tokens, width)
        return x.transpose(3, 0, 1, 2, 4).reshape(tokens, resp_count, query_heads, width)

    query_grad = from_rows(dqs)
    key_grad = jnp.stack(key_outs).transpose(2, 0, 1, 3)
    value_grad = jnp.stack(value_outs).transpose(2, 0, 1, 3)

    share = dprompt[0].astype(F32)
    for s in range(1, zs):
        share = share + shift(dprompt[s], -s, True).astype(F32)
    share = share[0] + swap(share[1].astype(BF16)).astype(F32)
    step = 1
    while step < group_size:
        pairs = [(i, i ^ step) for i in range(group_size)]
        share = share + lax.ppermute(share, "group", pairs)
        step *= 2
    low = share.astype(BF16).transpose(1, 2, 0, 3).reshape(2, prows, kv_heads * width)
    projected = dot_nt(low[0], key_matrix) + dot_nt(low[1], value_matrix)
    tensor = lax.axis_index("tensor")
    half = projected.shape[1] // 2
    mine = lax.dynamic_slice_in_dim(projected, tensor * half, half, 1)
    away = lax.dynamic_slice_in_dim(projected, (1 - tensor) * half, half, 1).astype(BF16)
    got = lax.ppermute(away, "tensor", [(0, 1), (1, 0)])
    prompt_input_grad = (mine + got.astype(F32)).astype(BF16)
    return (query_grad, key_grad, value_grad, prompt_input_grad)


def solution(mesh):
    placed = P("prefix", "group", "tensor", None)
    return jax.shard_map(
        per_device,
        mesh=mesh,
        in_specs=(
            placed,
            placed,
            placed,
            placed,
            P("prefix", "tensor", None),
            P("prefix", "tensor", None),
            P(None, "tensor"),
            P(None, "tensor"),
            P(),
        ),
        out_specs=(placed, placed, placed, P("prefix", "tensor")),
        check_vma=False,
    )
```

```python
import functools
import math

import jax
import jax.numpy as jnp
from jax import lax
from jax.experimental import pallas as pl
from jax.experimental.pallas import tpu as pltpu
from jax.sharding import PartitionSpec as P

MASKED = -1e30
F32 = jnp.float32
BF16 = jnp.bfloat16


def dot_nt(a, b):
    return lax.dot_general(a, b, (((1,), (1,)), ((), ())), preferred_element_type=F32)


def dot_nn(a, b):
    return lax.dot_general(a, b, (((1,), (0,)), ((), ())), preferred_element_type=F32)


def dot_tn(a, b):
    return lax.dot_general(a, b, (((0,), (0,)), ((), ())), preferred_element_type=F32)


def attention_kernel(tokens, prows, zs, last, meta, *refs):
    refs = list(refs)
    qd_refs = [refs.pop(0) for _ in range(2)]
    kv_refs = [refs.pop(0) for _ in range(zs)]
    pkv_refs = [refs.pop(0) for _ in range(zs)]
    prev_refs = [refs.pop(0) for _ in range(zs)] if last else None
    dq_refs = [refs.pop(0) for _ in range(2)]
    dkv_refs = [refs.pop(0) for _ in range(zs)]
    dpkv_refs = [refs.pop(0) for _ in range(zs)]
    e_ref, dp_ref, m_ref, l_ref, a_ref, mc_ref, dqt_ref, dk_acc, dv_acc = refs
    rows, width = qd_refs[0].shape[1:]
    scale = 1.0 / math.sqrt(width)
    log2 = scale * math.log2(math.e)
    z, xh = meta[0], meta[1]
    chunk = 2 * tokens
    pchunk = 4 * prows
    pcount = zs // 2
    pbase = 4 * tokens

    def prompt_pair(c, which):
        first = pbase + which * 2 * prows
        parts = [pkv_refs[2 * c + i][first : first + 2 * prows] for i in range(2)]
        return jnp.concatenate(parts, axis=0)

    def resp_pair(s, which):
        return kv_refs[s][which * chunk : (which + 1) * chunk]

    def forward(q, do, keys, values, base, index, mask):
        n = keys.shape[0]
        scores = dot_nt(keys, q)
        if mask is not None:
            scores = jnp.where(mask, scores, MASKED)
        top = jnp.max(scores, axis=0, keepdims=True)
        if index > 0:
            old = m_ref[...]
            top = jnp.maximum(old, top)
        e = jnp.exp2((scores - top) * log2)
        dp = dot_nt(values, do)
        esum = jnp.sum(e, axis=0, keepdims=True)
        dsum = jnp.sum(e * dp, axis=0, keepdims=True)
        if index > 0:
            fix = jnp.exp2((old - top) * log2)
            esum = esum + l_ref[...] * fix
            dsum = dsum + a_ref[...] * fix
        m_ref[...] = top
        l_ref[...] = esum
        a_ref[...] = dsum
        mc_ref[index] = top
        e_ref[base : base + n] = e
        dp_ref[base : base + n] = dp

    def backward(half, q, do, keys, base, index):
        n = keys.shape[0]
        inv = 1.0 / l_ref[...]
        factor = jnp.exp2((mc_ref[index] - m_ref[...]) * log2) * inv
        delta = a_ref[...] * inv
        p = e_ref[base : base + n] * factor
        ds = (p * (dp_ref[base : base + n] - delta)).astype(BF16)
        dv = dot_nn(p.astype(BF16), do)
        dk = dot_nn(ds, q)
        dqt = dot_tn(keys, ds)
        if index == 0:
            dqt_ref[...] = dqt
        else:
            dqt_ref[...] += dqt
        if half == 0:
            dk_acc[base : base + n] = dk
            dv_acc[base : base + n] = dv
        else:
            dk_acc[base : base + n] += dk
            dv_acc[base : base + n] += dv

    def when_past(s, step):
        if s == 0:
            step()
        else:
            pl.when(z >= s)(step)

    def one_half(half):
        q, do = qd_refs[half][0], qd_refs[half][1]
        for c in range(pcount):
            forward(q, do, prompt_pair(c, 0), prompt_pair(c, 1), c * pchunk, c, None)
        for s in range(zs):

            def step(s=s):
                mask = None
                if s == 0:
                    row = lax.broadcasted_iota(jnp.int32, (chunk, rows), 0)
                    lane = lax.broadcasted_iota(jnp.int32, (chunk, rows), 1)
                    slot = row // tokens
                    key_pos = (slot + xh - 2 * slot * xh) * tokens + lax.rem(row, tokens)
                    start = (1 - xh) if half else xh
                    mask = key_pos <= start * tokens + lax.rem(lane, tokens)
                base = pcount * pchunk + s * chunk
                forward(q, do, resp_pair(s, 0), resp_pair(s, 1), base, pcount + s, mask)

            when_past(s, step)
        for c in range(pcount):
            backward(half, q, do, prompt_pair(c, 0), c * pchunk, c)
        for s in range(zs):

            def step(s=s):
                base = pcount * pchunk + s * chunk
                backward(half, q, do, resp_pair(s, 0), base, pcount + s)

            when_past(s, step)
        dq_refs[half][...] = (dqt_ref[...] * scale).T.astype(BF16)

    for half in range(2):
        live = meta[2 + half]

        @pl.when(live > 0)
        def _(half=half):
            one_half(half)

        @pl.when(live <= 0)
        def _(half=half):
            dq_refs[half][...] = jnp.zeros_like(dq_refs[half])
            if half == 0:
                dk_acc[...] = jnp.zeros_like(dk_acc)
                dv_acc[...] = jnp.zeros_like(dv_acc)

    for s in range(zs):
        rows_s = 2 * prows
        for which, acc in ((0, dk_acc), (1, dv_acc)):
            term = acc[s * rows_s : (s + 1) * rows_s]
            if which == 0:
                term = term * scale
            span = slice(which * rows_s, (which + 1) * rows_s)
            if last:
                term = term + prev_refs[s][span]
            dpkv_refs[s][span] = term.astype(dpkv_refs[s].dtype)

    for s in range(zs):

        def store(s=s):
            base = pcount * pchunk + s * chunk
            dkv_refs[s][0:chunk] = (dk_acc[base : base + chunk] * scale).astype(BF16)
            dkv_refs[s][chunk : 2 * chunk] = dv_acc[base : base + chunk].astype(BF16)

        when_past(s, store)


def attention(meta, qds, kvs, pkvs, prev, tokens, prows):
    zs = len(kvs)
    last = prev is not None
    rows, width = qds[0].shape[1:]
    total = zs * 2 * (prows + tokens)
    in_vmem = pl.BlockSpec(memory_space=pltpu.VMEM)
    args = list(qds) + list(kvs) + list(pkvs) + (list(prev) if last else [])
    out_shape = (
        [jax.ShapeDtypeStruct((rows, width), BF16)] * 2
        + [jax.ShapeDtypeStruct((4 * tokens, width), BF16)] * zs
        + [jax.ShapeDtypeStruct((4 * prows, width), BF16 if last else F32)] * zs
    )
    scratch = [
        pltpu.VMEM((total, rows), F32),
        pltpu.VMEM((total, rows), F32),
        pltpu.VMEM((1, rows), F32),
        pltpu.VMEM((1, rows), F32),
        pltpu.VMEM((1, rows), F32),
        pltpu.VMEM((zs // 2 + zs, 1, rows), F32),
        pltpu.VMEM((width, rows), F32),
        pltpu.VMEM((total, width), F32),
        pltpu.VMEM((total, width), F32),
    ]
    return pl.pallas_call(
        functools.partial(attention_kernel, tokens, prows, zs, last),
        out_shape=out_shape,
        in_specs=[pl.BlockSpec(memory_space=pltpu.SMEM)] + [in_vmem] * len(args),
        out_specs=[in_vmem] * len(out_shape),
        scratch_shapes=scratch,
        compiler_params=pltpu.CompilerParams(vmem_limit_bytes=28 * 1024 * 1024),
        cost_estimate=pl.CostEstimate(
            flops=20 * rows * total * width,
            bytes_accessed=4 * 1024 * 1024,
            transcendentals=2 * rows * total,
        ),
        name="attention_grad",
    )(meta, *args)


def per_device(
    resp_query,
    response_key,
    response_value,
    resp_cotangent,
    prompt_key,
    prompt_value_rows,
    key_matrix,
    value_matrix,
    resp_lengths,
):
    tokens, resp_count, query_heads, width = resp_query.shape
    kv_heads = response_key.shape[2]
    factor = query_heads // kv_heads
    prows = prompt_key.shape[0]
    prefix_size = lax.axis_size("prefix")
    group_size = lax.axis_size("group")
    zs = prefix_size // 2
    prefix = lax.axis_index("prefix")
    z, xh = prefix // 2, prefix % 2
    first = xh == 0

    def swap(x):
        return lax.ppermute(x, "prefix", [(i, i ^ 1) for i in range(prefix_size)])

    def shift(x, s, wrap):
        pairs = [(i, i + 2 * s) for i in range(prefix_size)]
        if wrap:
            pairs = [(i, j % prefix_size) for i, j in pairs]
        else:
            pairs = [(i, j) for i, j in pairs if 0 <= j < prefix_size]
        return lax.ppermute(x, "prefix", pairs)

    def own_away(lo, hi):
        return jnp.where(first, lo, hi), jnp.where(first, hi, lo)

    def in_order(own, other):
        return jnp.where(first, own, other), jnp.where(first, other, own)

    resp = jnp.stack((response_key, response_value), 0).transpose(3, 2, 0, 1, 4)
    prompt = jnp.stack((prompt_key, prompt_value_rows), 0).transpose(2, 0, 1, 3)
    resp_own, resp_away = own_away(resp[0], resp[1])
    prompt_own, prompt_away = own_away(prompt[0], prompt[1])
    flat = jnp.concatenate((resp_away.reshape(-1, width), prompt_away.reshape(-1, width)))
    got = swap(flat)
    split = resp_away.size // width
    resp_got = got[:split].reshape(resp_own.shape)
    prompt_got = got[split:].reshape(prompt_own.shape)
    resp_pair = jnp.stack((resp_own, resp_got), 2).reshape(resp_count, 4 * tokens, width)
    prompt_pair = jnp.stack((prompt_own, prompt_got), 1).reshape(4 * prows, width)

    position = prefix * tokens + jnp.arange(tokens, dtype=jnp.int32)
    own_lengths = lax.dynamic_slice_in_dim(
        resp_lengths, lax.axis_index("group") * resp_count, resp_count
    )
    live_rows = position[:, None] < own_lengths[None, :]
    cot = jnp.where(live_rows[:, :, None, None], resp_cotangent, jnp.zeros_like(resp_cotangent))

    qds = []
    for r in range(resp_count):
        pair = jnp.stack((resp_query[:, r], cot[:, r]), 0)
        own, away = own_away(pair[:, :, :factor], pair[:, :, factor:])
        own = own.transpose(0, 2, 1, 3).reshape(2, factor * tokens, width)
        away = away.transpose(0, 2, 1, 3).reshape(2, factor * tokens, width)
        qds.append((own, swap(away)))

    kvs = []
    for r in range(resp_count):
        message = resp_pair[r]
        if r == 0:
            message = jnp.concatenate((message, prompt_pair))
        kvs.append([message] + [shift(message, s, r == 0) for s in range(1, zs)])
    pkvs = kvs[0]

    dqs, totals = [], []
    dprompt = None
    for r in range(resp_count):
        live = [own_lengths[r] > (2 * z + place) * tokens for place in (xh, 1 - xh)]
        meta = jnp.stack([z, xh] + live).astype(jnp.int32)
        outs = list(attention(meta, qds[r], kvs[r], pkvs, dprompt, tokens, prows))
        dqs.append((outs[0], swap(outs[1])))
        dkv = outs[2 : 2 + zs]
        dprompt = outs[2 + zs :]
        total = dkv[0].astype(F32)
        for s in range(1, zs):
            total = total + shift(dkv[s], -s, False).astype(F32)
        totals.append(total.reshape(2, 2, tokens, width).astype(BF16))
    total = jnp.stack(totals)
    grads = in_order(total[:, :, 0], swap(total[:, :, 1]))
    grads = jnp.stack(grads, 2).transpose(1, 3, 0, 2, 4)

    query_grad = []
    for own, other in dqs:
        pair = [x.reshape(factor, tokens, width) for x in in_order(own, other)]
        query_grad.append(jnp.concatenate(pair, 0))
    query_grad = jnp.stack(query_grad).transpose(2, 0, 1, 3)

    share = dprompt[0].astype(F32)
    for s in range(1, zs):
        share = share + shift(dprompt[s], -s, True).astype(F32)

    def exchange(x, step):
        return lax.ppermute(x, "group", [(i, i ^ step) for i in range(group_size)])

    share = (share + exchange(share, 1)).astype(BF16)
    terms = [share] + [exchange(share, step) for step in range(2, group_size, 2)]
    terms = [x.astype(F32) for x in terms]
    while len(terms) > 1:
        terms = [terms[i] + terms[i + 1] for i in range(0, len(terms), 2)]
    low = terms[0].astype(BF16).reshape(2, 2, prows, width)
    low = jnp.concatenate(in_order(low[:, 0], swap(low[:, 1])), 2)
    projected = dot_nt(low[0], key_matrix) + dot_nt(low[1], value_matrix)
    tensor = lax.axis_index("tensor")
    half = projected.shape[1] // 2
    mine = lax.dynamic_slice_in_dim(projected, tensor * half, half, 1)
    away = lax.dynamic_slice_in_dim(projected, (1 - tensor) * half, half, 1).astype(BF16)
    got = lax.ppermute(away, "tensor", [(0, 1), (1, 0)])
    prompt_input_grad = (mine + got.astype(F32)).astype(BF16)
    return (query_grad, grads[0], grads[1], prompt_input_grad)


def solution(mesh):
    placed = P("prefix", "group", "tensor", None)
    return jax.shard_map(
        per_device,
        mesh=mesh,
        in_specs=(
            placed,
            placed,
            placed,
            placed,
            P("prefix", "tensor", None),
            P("prefix", "tensor", None),
            P(None, "tensor"),
            P(None, "tensor"),
            P(),
        ),
        out_specs=(placed, placed, placed, P("prefix", "tensor")),
        check_vma=False,
    )
```

```python
import functools
import math

import jax
import jax.numpy as jnp
from jax import lax
from jax.experimental import pallas as pl
from jax.experimental.pallas import tpu as pltpu
from jax.sharding import PartitionSpec as P

MASKED = -1e30
F32 = jnp.float32
BF16 = jnp.bfloat16


def dot_nt(a, b):
    return lax.dot_general(a, b, (((1,), (1,)), ((), ())), preferred_element_type=F32)


def dot_nn(a, b):
    return lax.dot_general(a, b, (((1,), (0,)), ((), ())), preferred_element_type=F32)


def dot_tn(a, b):
    return lax.dot_general(a, b, (((0,), (0,)), ((), ())), preferred_element_type=F32)


def attention_kernel(tokens, prows, zs, count, meta, *refs):
    refs = list(refs)
    qd_hbm = [[refs.pop(0) for _ in range(2)] for _ in range(count)]
    kv_refs = [refs.pop(0) for _ in range(zs)]
    dq_hbm = [refs.pop(0) for _ in range(2)]
    dkv_hbm = [refs.pop(0) for _ in range(zs)]
    dpkv_hbm = [refs.pop(0) for _ in range(zs)]
    e_ref, dp_ref, m_ref, l_ref, a_ref, mc_ref, dqt_ref, dk_acc, dv_acc = refs[:9]
    qd_refs, dq_refs, dkv_refs, dpkv_ref, in_sem, dq_sem, dkv_sem, dpkv_sem = refs[9:]
    rows, width = qd_refs.shape[3:]

    def incoming(r, half, source=0):
        return pltpu.make_async_copy(qd_hbm[source][half], qd_refs.at[r, half], in_sem.at[r, half])

    def dq_out(r, half):
        return pltpu.make_async_copy(dq_refs.at[r, half], dq_hbm[half].at[r], dq_sem.at[r, half])

    def dkv_out(r, s):
        return pltpu.make_async_copy(dkv_refs.at[r, s], dkv_hbm[s].at[r], dkv_sem.at[r, s])

    def dpkv_out(s):
        return pltpu.make_async_copy(dpkv_ref.at[s], dpkv_hbm[s], dpkv_sem.at[s])

    for r in range(count):
        for half in range(2):
            incoming(r, half, r).start()
    scale = 1.0 / math.sqrt(width)
    log2 = scale * math.log2(math.e)
    z, xh = meta[0], meta[1]
    chunk = 2 * tokens
    pchunk = 4 * prows
    pcount = zs // 2
    pbase = 4 * tokens * count
    prompt_rows = pcount * pchunk

    def prompt_pair(c, which):
        first = pbase + which * 2 * prows
        parts = [kv_refs[2 * c + i][first : first + 2 * prows] for i in range(2)]
        return jnp.concatenate(parts, axis=0)

    def resp_pair(r, s, which):
        first = pl.multiple_of(r * (4 * tokens) + which * chunk, chunk)
        return kv_refs[s][pl.ds(first, chunk)]

    def forward(q, do, keys, values, base, index, mask):
        n = keys.shape[0]
        scores = dot_nt(keys, q)
        if mask is not None:
            scores = jnp.where(mask, scores, MASKED)
        top = jnp.max(scores, axis=0, keepdims=True)
        if index > 0:
            old = m_ref[...]
            top = jnp.maximum(old, top)
        e = jnp.exp2((scores - top) * log2)
        dp = dot_nt(values, do)
        esum = jnp.sum(e, axis=0, keepdims=True)
        dsum = jnp.sum(e * dp, axis=0, keepdims=True)
        if index > 0:
            fix = jnp.exp2((old - top) * log2)
            esum = esum + l_ref[...] * fix
            dsum = dsum + a_ref[...] * fix
        m_ref[...] = top
        l_ref[...] = esum
        a_ref[...] = dsum
        mc_ref[index] = top
        e_ref[base : base + n] = e
        dp_ref[base : base + n] = dp

    def backward(half, q, do, keys, base, index):
        n = keys.shape[0]
        inv = 1.0 / l_ref[...]
        factor = jnp.exp2((mc_ref[index] - m_ref[...]) * log2) * inv
        delta = a_ref[...] * inv
        p = e_ref[base : base + n] * factor
        ds = (p * (dp_ref[base : base + n] - delta)).astype(BF16)
        dv = dot_nn(p.astype(BF16), do)
        dk = dot_nn(ds, q)
        dqt = dot_tn(keys, ds)
        if index == 0:
            dqt_ref[...] = dqt
        else:
            dqt_ref[...] += dqt
        if half == 0 and base >= prompt_rows:
            dk_acc[base : base + n] = dk
            dv_acc[base : base + n] = dv
        else:
            dk_acc[base : base + n] += dk
            dv_acc[base : base + n] += dv

    def when_past(s, step):
        if s == 0:
            step()
        else:
            pl.when(z >= s)(step)

    def one_half(r, half):
        token = lax.rem(lax.broadcasted_iota(jnp.int32, (rows, width), 0), tokens)
        raw = qd_refs[r, half, 1].astype(F32)
        qd_refs[r, half, 1] = jnp.where(token < meta[2 + 2 * r + half], raw, 0.0).astype(BF16)
        q, do = qd_refs[r, half, 0], qd_refs[r, half, 1]
        for c in range(pcount):
            forward(q, do, prompt_pair(c, 0), prompt_pair(c, 1), c * pchunk, c, None)
        for s in range(zs):

            def step(s=s):
                mask = None
                if s == 0:
                    row = lax.broadcasted_iota(jnp.int32, (chunk, rows), 0)
                    lane = lax.broadcasted_iota(jnp.int32, (chunk, rows), 1)
                    slot = row // tokens
                    key_pos = (slot + xh - 2 * slot * xh) * tokens + lax.rem(row, tokens)
                    start = (1 - xh) if half else xh
                    mask = key_pos <= start * tokens + lax.rem(lane, tokens)
                base = pcount * pchunk + s * chunk
                forward(q, do, resp_pair(r, s, 0), resp_pair(r, s, 1), base, pcount + s, mask)

            when_past(s, step)
        for c in range(pcount):
            backward(half, q, do, prompt_pair(c, 0), c * pchunk, c)
        for s in range(zs):

            def step(s=s):
                base = pcount * pchunk + s * chunk
                backward(half, q, do, resp_pair(r, s, 0), base, pcount + s)

            when_past(s, step)
        dq_refs[r, half] = (dqt_ref[...] * scale).T.astype(BF16)

    dk_acc[0:prompt_rows] = jnp.zeros((prompt_rows, width), F32)
    dv_acc[0:prompt_rows] = jnp.zeros((prompt_rows, width), F32)

    @pl.loop(0, count)
    def _(r):
        for half in range(2):
            live = meta[2 + 2 * r + half]
            incoming(r, half).wait()

            @pl.when(live > 0)
            def _(half=half):
                one_half(r, half)

            @pl.when(live <= 0)
            def _(half=half):
                dq_refs[r, half] = jnp.zeros((rows, width), BF16)
                if half == 0:
                    zeros = jnp.zeros((dk_acc.shape[0] - prompt_rows, width), F32)
                    dk_acc[prompt_rows:] = zeros
                    dv_acc[prompt_rows:] = zeros

            dq_out(r, half).start()

        for s in range(zs):

            def store(s=s):
                base = prompt_rows + s * chunk
                dkv_refs[r, s, 0:chunk] = (dk_acc[base : base + chunk] * scale).astype(BF16)
                dkv_refs[r, s, chunk : 2 * chunk] = dv_acc[base : base + chunk].astype(BF16)
                dkv_out(r, s).start()

            when_past(s, store)

    for s in range(zs):
        n = 2 * prows
        span = slice(s * n, (s + 1) * n)
        dpkv_ref[s, 0:n] = (dk_acc[span] * scale).astype(BF16)
        dpkv_ref[s, n : 2 * n] = dv_acc[span].astype(BF16)
        dpkv_out(s).start()
    for s in range(zs):
        dpkv_out(s).wait()
    for r in range(count):
        for half in range(2):
            dq_out(r, half).wait()
        for s in range(zs):
            when_past(s, dkv_out(r, s).wait)


def attention(meta, qds, kvs, count, tokens, prows):
    zs = len(kvs)
    rows, width = qds[0].shape[1:]
    total = zs * 2 * (prows + tokens)
    in_vmem = pl.BlockSpec(memory_space=pltpu.VMEM)
    in_hbm = pl.BlockSpec(memory_space=pltpu.HBM)
    args = [pltpu.with_memory_space_constraint(x, pltpu.HBM) for x in qds] + list(kvs)
    in_specs = [pl.BlockSpec(memory_space=pltpu.SMEM)] + [in_hbm] * len(qds) + [in_vmem] * zs
    out_shape = [pltpu.HBM((count, rows, width), BF16)] * 2
    out_shape += [pltpu.HBM((count, 4 * tokens, width), BF16)] * zs
    out_shape += [pltpu.HBM((4 * prows, width), BF16)] * zs
    scratch = [
        pltpu.VMEM((total, rows), F32),
        pltpu.VMEM((total, rows), F32),
        pltpu.VMEM((1, rows), F32),
        pltpu.VMEM((1, rows), F32),
        pltpu.VMEM((1, rows), F32),
        pltpu.VMEM((zs // 2 + zs, 1, rows), F32),
        pltpu.VMEM((width, rows), F32),
        pltpu.VMEM((total, width), F32),
        pltpu.VMEM((total, width), F32),
        pltpu.VMEM((count, 2, 2, rows, width), BF16),
        pltpu.VMEM((count, 2, rows, width), BF16),
        pltpu.VMEM((count, zs, 4 * tokens, width), BF16),
        pltpu.VMEM((zs, 4 * prows, width), BF16),
        pltpu.SemaphoreType.DMA((count, 2)),
        pltpu.SemaphoreType.DMA((count, 2)),
        pltpu.SemaphoreType.DMA((count, zs)),
        pltpu.SemaphoreType.DMA((zs,)),
    ]
    return pl.pallas_call(
        functools.partial(attention_kernel, tokens, prows, zs, count),
        out_shape=out_shape,
        in_specs=in_specs,
        out_specs=[in_hbm] * len(out_shape),
        scratch_shapes=scratch,
        compiler_params=pltpu.CompilerParams(vmem_limit_bytes=30 * 1024 * 1024),
        cost_estimate=pl.CostEstimate(
            flops=20 * count * rows * total * width,
            bytes_accessed=8 * 1024 * 1024,
            transcendentals=2 * count * rows * total,
        ),
        name="attention_grad",
    )(meta, *args)


def per_device(
    resp_query,
    response_key,
    response_value,
    resp_cotangent,
    prompt_key,
    prompt_value_rows,
    key_matrix,
    value_matrix,
    resp_lengths,
):
    tokens, resp_count, query_heads, width = resp_query.shape
    kv_heads = response_key.shape[2]
    factor = query_heads // kv_heads
    prows = prompt_key.shape[0]
    prefix_size = lax.axis_size("prefix")
    group_size = lax.axis_size("group")
    zs = prefix_size // 2
    prefix = lax.axis_index("prefix")
    z, xh = prefix // 2, prefix % 2
    first = xh == 0

    def swap(x):
        return lax.ppermute(x, "prefix", [(i, i ^ 1) for i in range(prefix_size)])

    def shift(x, s, wrap):
        pairs = [(i, i + 2 * s) for i in range(prefix_size)]
        if wrap:
            pairs = [(i, j % prefix_size) for i, j in pairs]
        else:
            pairs = [(i, j) for i, j in pairs if 0 <= j < prefix_size]
        return lax.ppermute(x, "prefix", pairs)

    def own_away(lo, hi):
        return jnp.where(first, lo, hi), jnp.where(first, hi, lo)

    def in_order(own, other):
        return jnp.where(first, own, other), jnp.where(first, other, own)

    resp = jnp.stack((response_key, response_value), 0).transpose(3, 2, 0, 1, 4)
    prompt = jnp.stack((prompt_key, prompt_value_rows), 0).transpose(2, 0, 1, 3)
    resp_own, resp_away = own_away(resp[0], resp[1])
    prompt_own, prompt_away = own_away(prompt[0], prompt[1])
    flat = jnp.concatenate((resp_away.reshape(-1, width), prompt_away.reshape(-1, width)))
    got = swap(flat)
    split = resp_away.size // width
    resp_got = got[:split].reshape(resp_own.shape)
    prompt_got = got[split:].reshape(prompt_own.shape)
    resp_pair = jnp.stack((resp_own, resp_got), 2).reshape(resp_count, 4 * tokens, width)
    prompt_pair = jnp.stack((prompt_own, prompt_got), 1).reshape(4 * prows, width)

    own_lengths = lax.dynamic_slice_in_dim(
        resp_lengths, lax.axis_index("group") * resp_count, resp_count
    )

    message = jnp.concatenate((resp_pair.reshape(-1, width), prompt_pair))
    kvs = [message] + [shift(message, s, True) for s in range(1, zs)]

    qds = []
    for r in range(resp_count):
        pair = jnp.stack((resp_query[:, r], resp_cotangent[:, r]), 0)
        own, away = own_away(pair[:, :, :factor], pair[:, :, factor:])
        own = own.transpose(0, 2, 1, 3).reshape(2, factor * tokens, width)
        away = away.transpose(0, 2, 1, 3).reshape(2, factor * tokens, width)
        qds += [own, swap(away)]

    live = [
        own_lengths[r] - (2 * z + place) * tokens
        for r in range(resp_count)
        for place in (xh, 1 - xh)
    ]
    meta = jnp.stack([z, xh] + live).astype(jnp.int32)
    outs = list(attention(meta, qds, kvs, resp_count, tokens, prows))
    dq_own, dq_away = outs[:2]
    dkv = outs[2 : 2 + zs]
    dprompt = outs[2 + zs :]

    def exchange(x, step):
        return lax.ppermute(x, "group", [(i, i ^ step) for i in range(group_size)])

    share = dprompt[0].astype(F32)
    for s in range(1, zs):
        share = share + shift(dprompt[s], -s, True).astype(F32)
    dq_got = swap(dq_away)
    share = (share + exchange(share, 1)).astype(BF16)
    terms = [share] + [exchange(share, step) for step in range(2, group_size, 2)]
    terms[1], dkv[1] = lax.optimization_barrier((terms[1], dkv[1]))
    near = shift(dkv[1], -1, False)
    *terms, dq_got = lax.optimization_barrier((*terms, dq_got))
    terms = [x.astype(F32) for x in terms]
    while len(terms) > 1:
        terms = [terms[i] + terms[i + 1] for i in range(0, len(terms), 2)]
    share, *dkv[2:] = lax.optimization_barrier((terms[0].astype(BF16), *dkv[2:]))
    low = share.reshape(2, 2, prows, width)
    low = jnp.concatenate(in_order(low[:, 0], swap(low[:, 1])), 2)
    projected = dot_nt(low[0], key_matrix) + dot_nt(low[1], value_matrix)

    total = dkv[0].astype(F32) + near.astype(F32)
    for s in range(2, zs):
        total = total + shift(dkv[s], -s, False).astype(F32)
    total = total.reshape(resp_count, 2, 2, tokens, width).astype(BF16)
    grads = in_order(total[:, :, 0], swap(total[:, :, 1]))
    grads = jnp.stack(grads, 2).transpose(1, 3, 0, 2, 4)

    tensor = lax.axis_index("tensor")
    half = projected.shape[1] // 2
    mine = lax.dynamic_slice_in_dim(projected, tensor * half, half, 1)
    away = lax.dynamic_slice_in_dim(projected, (1 - tensor) * half, half, 1).astype(BF16)
    away, dq_got = lax.optimization_barrier((away, dq_got))
    pair = [x.reshape(resp_count, factor, tokens, width) for x in in_order(dq_own, dq_got)]
    query_grad = jnp.concatenate(pair, 1).transpose(2, 0, 1, 3)
    got = lax.ppermute(away, "tensor", [(0, 1), (1, 0)])
    prompt_input_grad = (mine + got.astype(F32)).astype(BF16)
    return (query_grad, grads[0], grads[1], prompt_input_grad)


def solution(mesh):
    placed = P("prefix", "group", "tensor", None)
    return jax.shard_map(
        per_device,
        mesh=mesh,
        in_specs=(
            placed,
            placed,
            placed,
            placed,
            P("prefix", "tensor", None),
            P("prefix", "tensor", None),
            P(None, "tensor"),
            P(None, "tensor"),
            P(),
        ),
        out_specs=(placed, placed, placed, P("prefix", "tensor")),
        check_vma=False,
    )
```

```python
import functools
import math

import jax
import jax.numpy as jnp
from jax import lax
from jax.experimental import pallas as pl
from jax.experimental.pallas import tpu as pltpu
from jax.sharding import PartitionSpec as P

MASKED = -1e30
F32 = jnp.float32
BF16 = jnp.bfloat16


def dot_nt(a, b):
    return lax.dot_general(a, b, (((1,), (1,)), ((), ())), preferred_element_type=F32)


def dot_nn(a, b):
    return lax.dot_general(a, b, (((1,), (0,)), ((), ())), preferred_element_type=F32)


def dot_tn(a, b):
    return lax.dot_general(a, b, (((0,), (0,)), ((), ())), preferred_element_type=F32)


def attention_kernel(tokens, prows, zs, count, meta, *refs):
    refs = list(refs)
    qd_hbm = [[refs.pop(0) for _ in range(2)] for _ in range(count)]
    kv_refs = [refs.pop(0) for _ in range(zs)]
    dq_hbm = [refs.pop(0) for _ in range(2)]
    dkv_hbm = [refs.pop(0) for _ in range(zs)]
    dpkv_hbm = [refs.pop(0) for _ in range(zs)]
    e_ref, dp_ref, m_ref, l_ref, a_ref, mc_ref, dqt_ref, dk_acc, dv_acc = refs[:9]
    qd_refs, dq_refs, dkv_refs, dpkv_ref, in_sem, dq_sem, dkv_sem, dpkv_sem = refs[9:]
    rows, width = qd_refs.shape[3:]

    def incoming(r, half, source=0):
        return pltpu.make_async_copy(qd_hbm[source][half], qd_refs.at[r, half], in_sem.at[r, half])

    def dq_out(r, half):
        return pltpu.make_async_copy(dq_refs.at[r, half], dq_hbm[half].at[r], dq_sem.at[r, half])

    def dkv_out(r, s):
        return pltpu.make_async_copy(dkv_refs.at[r, s], dkv_hbm[s].at[r], dkv_sem.at[r, s])

    def dpkv_out(s):
        return pltpu.make_async_copy(dpkv_ref.at[s], dpkv_hbm[s], dpkv_sem.at[s])

    for r in range(count):
        for half in range(2):
            incoming(r, half, r).start()
    scale = 1.0 / math.sqrt(width)
    log2 = scale * math.log2(math.e)
    z, xh = meta[0], meta[1]
    chunk = 2 * tokens
    pchunk = 4 * prows
    pcount = zs // 2
    pbase = 4 * tokens * count
    prompt_rows = pcount * pchunk

    def prompt_pair(c, which):
        first = pbase + which * 2 * prows
        parts = [kv_refs[2 * c + i][first : first + 2 * prows] for i in range(2)]
        return jnp.concatenate(parts, axis=0)

    def resp_pair(r, s, which):
        first = pl.multiple_of(r * (4 * tokens) + which * chunk, chunk)
        return kv_refs[s][pl.ds(first, chunk)]

    def forward(q, do, keys, values, base, index, mask):
        n = keys.shape[0]
        scores = dot_nt(keys, q)
        if mask is not None:
            scores = jnp.where(mask, scores, MASKED)
        top = jnp.max(scores, axis=0, keepdims=True)
        if index > 0:
            old = m_ref[...]
            top = jnp.maximum(old, top)
        e = jnp.exp2((scores - top) * log2)
        dp = dot_nt(values, do)
        esum = jnp.sum(e, axis=0, keepdims=True)
        dsum = jnp.sum(e * dp, axis=0, keepdims=True)
        if index > 0:
            fix = jnp.exp2((old - top) * log2)
            esum = esum + l_ref[...] * fix
            dsum = dsum + a_ref[...] * fix
        m_ref[...] = top
        l_ref[...] = esum
        a_ref[...] = dsum
        mc_ref[index] = top
        e_ref[base : base + n] = e
        dp_ref[base : base + n] = dp

    def backward(half, q, do, keys, base, index):
        n = keys.shape[0]
        inv = 1.0 / l_ref[...]
        factor = jnp.exp2((mc_ref[index] - m_ref[...]) * log2) * inv
        delta = a_ref[...] * inv
        p = e_ref[base : base + n] * factor
        ds = (p * (dp_ref[base : base + n] - delta)).astype(BF16)
        dv = dot_nn(p.astype(BF16), do)
        dk = dot_nn(ds, q)
        dqt = dot_tn(keys, ds)
        if index == 0:
            dqt_ref[...] = dqt
        else:
            dqt_ref[...] += dqt
        if half == 0 and base >= prompt_rows:
            dk_acc[base : base + n] = dk
            dv_acc[base : base + n] = dv
        else:
            dk_acc[base : base + n] += dk
            dv_acc[base : base + n] += dv

    def when_past(s, step):
        if s == 0:
            step()
        else:
            pl.when(z >= s)(step)

    def past_all(step):
        @pl.when(z == zs - 1)
        def _():
            for s in range(zs):
                step(s)

        @pl.when(z < zs - 1)
        def _():
            for s in range(zs):
                when_past(s, functools.partial(step, s))

    def one_half(r, half):
        token = lax.broadcasted_iota(jnp.int32, (rows, width), 0) & (tokens - 1)
        raw = qd_refs[r, half, 1].astype(F32)
        qd_refs[r, half, 1] = jnp.where(token < meta[2 + 2 * r + half], raw, 0.0).astype(BF16)
        q, do = qd_refs[r, half, 0], qd_refs[r, half, 1]
        for c in range(pcount):
            forward(q, do, prompt_pair(c, 0), prompt_pair(c, 1), c * pchunk, c, None)
        def forward_step(s):
            mask = None
            if s == 0:
                row = lax.broadcasted_iota(jnp.int32, (chunk, rows), 0)
                lane = lax.broadcasted_iota(jnp.int32, (1, rows), 1)
                start = (1 - xh) if half else xh
                token = (lane & (tokens - 1)) + start * tokens
                mask = (row ^ (xh * tokens)) <= token
            base = pcount * pchunk + s * chunk
            forward(q, do, resp_pair(r, s, 0), resp_pair(r, s, 1), base, pcount + s, mask)

        past_all(forward_step)
        for c in range(pcount):
            backward(half, q, do, prompt_pair(c, 0), c * pchunk, c)
        def backward_step(s):
            base = pcount * pchunk + s * chunk
            backward(half, q, do, resp_pair(r, s, 0), base, pcount + s)

        past_all(backward_step)
        dq_refs[r, half] = (dqt_ref[...] * scale).T.astype(BF16)

    dk_acc[0:prompt_rows] = jnp.zeros((prompt_rows, width), F32)
    dv_acc[0:prompt_rows] = jnp.zeros((prompt_rows, width), F32)

    @pl.loop(0, count)
    def _(r):
        for half in range(2):
            live = meta[2 + 2 * r + half]
            incoming(r, half).wait()

            @pl.when(live > 0)
            def _(half=half):
                one_half(r, half)

            @pl.when(live <= 0)
            def _(half=half):
                dq_refs[r, half] = jnp.zeros((rows, width), BF16)
                if half == 0:
                    zeros = jnp.zeros((dk_acc.shape[0] - prompt_rows, width), F32)
                    dk_acc[prompt_rows:] = zeros
                    dv_acc[prompt_rows:] = zeros

            dq_out(r, half).start()

        for s in range(zs):

            def store(s=s):
                base = prompt_rows + s * chunk
                dkv_refs[r, s, 0:chunk] = (dk_acc[base : base + chunk] * scale).astype(BF16)
                dkv_refs[r, s, chunk : 2 * chunk] = dv_acc[base : base + chunk].astype(BF16)
                dkv_out(r, s).start()

            when_past(s, store)

    for s in range(zs):
        n = 2 * prows
        span = slice(s * n, (s + 1) * n)
        dpkv_ref[s, 0:n] = (dk_acc[span] * scale).astype(BF16)
        dpkv_ref[s, n : 2 * n] = dv_acc[span].astype(BF16)
        dpkv_out(s).start()
    for s in range(zs):
        dpkv_out(s).wait()
    for r in range(count):
        for half in range(2):
            dq_out(r, half).wait()
        for s in range(zs):
            when_past(s, dkv_out(r, s).wait)


def attention(meta, qds, kvs, count, tokens, prows):
    zs = len(kvs)
    rows, width = qds[0].shape[1:]
    total = zs * 2 * (prows + tokens)
    in_vmem = pl.BlockSpec(memory_space=pltpu.VMEM)
    in_hbm = pl.BlockSpec(memory_space=pltpu.HBM)
    args = [pltpu.with_memory_space_constraint(x, pltpu.HBM) for x in qds] + list(kvs)
    in_specs = [pl.BlockSpec(memory_space=pltpu.SMEM)] + [in_hbm] * len(qds) + [in_vmem] * zs
    out_shape = [pltpu.HBM((count, rows, width), BF16)] * 2
    out_shape += [pltpu.HBM((count, 4 * tokens, width), BF16)] * zs
    out_shape += [pltpu.HBM((4 * prows, width), BF16)] * zs
    scratch = [
        pltpu.VMEM((total, rows), F32),
        pltpu.VMEM((total, rows), F32),
        pltpu.VMEM((1, rows), F32),
        pltpu.VMEM((1, rows), F32),
        pltpu.VMEM((1, rows), F32),
        pltpu.VMEM((zs // 2 + zs, 1, rows), F32),
        pltpu.VMEM((width, rows), F32),
        pltpu.VMEM((total, width), F32),
        pltpu.VMEM((total, width), F32),
        pltpu.VMEM((count, 2, 2, rows, width), BF16),
        pltpu.VMEM((count, 2, rows, width), BF16),
        pltpu.VMEM((count, zs, 4 * tokens, width), BF16),
        pltpu.VMEM((zs, 4 * prows, width), BF16),
        pltpu.SemaphoreType.DMA((count, 2)),
        pltpu.SemaphoreType.DMA((count, 2)),
        pltpu.SemaphoreType.DMA((count, zs)),
        pltpu.SemaphoreType.DMA((zs,)),
    ]
    return pl.pallas_call(
        functools.partial(attention_kernel, tokens, prows, zs, count),
        out_shape=out_shape,
        in_specs=in_specs,
        out_specs=[in_hbm] * len(out_shape),
        scratch_shapes=scratch,
        compiler_params=pltpu.CompilerParams(vmem_limit_bytes=30 * 1024 * 1024),
        cost_estimate=pl.CostEstimate(
            flops=20 * count * rows * total * width,
            bytes_accessed=8 * 1024 * 1024,
            transcendentals=2 * count * rows * total,
        ),
        name="attention_grad",
    )(meta, *args)


def per_device(
    resp_query,
    response_key,
    response_value,
    resp_cotangent,
    prompt_key,
    prompt_value_rows,
    key_matrix,
    value_matrix,
    resp_lengths,
):
    tokens, resp_count, query_heads, width = resp_query.shape
    kv_heads = response_key.shape[2]
    factor = query_heads // kv_heads
    prows = prompt_key.shape[0]
    prefix_size = lax.axis_size("prefix")
    group_size = lax.axis_size("group")
    zs = prefix_size // 2
    prefix = lax.axis_index("prefix")
    z, xh = prefix // 2, prefix % 2
    first = xh == 0

    def swap(x):
        return lax.ppermute(x, "prefix", [(i, i ^ 1) for i in range(prefix_size)])

    def shift(x, s, wrap):
        pairs = [(i, i + 2 * s) for i in range(prefix_size)]
        if wrap:
            pairs = [(i, j % prefix_size) for i, j in pairs]
        else:
            pairs = [(i, j) for i, j in pairs if 0 <= j < prefix_size]
        return lax.ppermute(x, "prefix", pairs)

    def own_away(lo, hi):
        return jnp.where(first, lo, hi), jnp.where(first, hi, lo)

    def in_order(own, other):
        return jnp.where(first, own, other), jnp.where(first, other, own)

    resp = jnp.stack((response_key, response_value), 0).transpose(3, 2, 0, 1, 4)
    prompt = jnp.stack((prompt_key, prompt_value_rows), 0).transpose(2, 0, 1, 3)
    resp_own, resp_away = own_away(resp[0], resp[1])
    prompt_own, prompt_away = own_away(prompt[0], prompt[1])
    flat = jnp.concatenate((resp_away.reshape(-1, width), prompt_away.reshape(-1, width)))
    got = swap(flat)
    split = resp_away.size // width
    resp_got = got[:split].reshape(resp_own.shape)
    prompt_got = got[split:].reshape(prompt_own.shape)
    resp_pair = jnp.stack((resp_own, resp_got), 2).reshape(resp_count, 4 * tokens, width)
    prompt_pair = jnp.stack((prompt_own, prompt_got), 1).reshape(4 * prows, width)

    own_lengths = lax.dynamic_slice_in_dim(
        resp_lengths, lax.axis_index("group") * resp_count, resp_count
    )

    message = jnp.concatenate((resp_pair.reshape(-1, width), prompt_pair))
    kvs = [message] + [shift(message, s, True) for s in range(1, zs)]

    qds = []
    for r in range(resp_count):
        pair = jnp.stack((resp_query[:, r], resp_cotangent[:, r]), 0)
        own, away = own_away(pair[:, :, :factor], pair[:, :, factor:])
        own = own.transpose(0, 2, 1, 3).reshape(2, factor * tokens, width)
        away = away.transpose(0, 2, 1, 3).reshape(2, factor * tokens, width)
        qds += [own, swap(away)]

    live = [
        own_lengths[r] - (2 * z + place) * tokens
        for r in range(resp_count)
        for place in (xh, 1 - xh)
    ]
    meta = jnp.stack([z, xh] + live).astype(jnp.int32)
    outs = list(attention(meta, qds, kvs, resp_count, tokens, prows))
    dq_own, dq_away = outs[:2]
    dkv = outs[2 : 2 + zs]
    dprompt = outs[2 + zs :]

    def exchange(x, step):
        return lax.ppermute(x, "group", [(i, i ^ step) for i in range(group_size)])

    share = dprompt[0].astype(F32)
    for s in range(1, zs):
        share = share + shift(dprompt[s], -s, True).astype(F32)
    dq_got = swap(dq_away)
    share = (share + exchange(share, 1)).astype(BF16)
    terms = [share] + [exchange(share, step) for step in range(2, group_size, 2)]
    terms[1], dkv[1] = lax.optimization_barrier((terms[1], dkv[1]))
    near = shift(dkv[1], -1, False)
    *terms, dq_got = lax.optimization_barrier((*terms, dq_got))
    terms = [x.astype(F32) for x in terms]
    while len(terms) > 1:
        terms = [terms[i] + terms[i + 1] for i in range(0, len(terms), 2)]
    share, *dkv[2:] = lax.optimization_barrier((terms[0].astype(BF16), *dkv[2:]))
    low = share.reshape(2, 2, prows, width)
    low = jnp.concatenate(in_order(low[:, 0], swap(low[:, 1])), 2)
    projected = dot_nt(low[0], key_matrix) + dot_nt(low[1], value_matrix)

    total = dkv[0].astype(F32) + near.astype(F32)
    for s in range(2, zs):
        total = total + shift(dkv[s], -s, False).astype(F32)
    total = total.reshape(resp_count, 2, 2, tokens, width).astype(BF16)
    grads = in_order(total[:, :, 0], swap(total[:, :, 1]))
    grads = jnp.stack(grads, 2).transpose(1, 3, 0, 2, 4)

    tensor = lax.axis_index("tensor")
    half = projected.shape[1] // 2
    mine = lax.dynamic_slice_in_dim(projected, tensor * half, half, 1)
    away = lax.dynamic_slice_in_dim(projected, (1 - tensor) * half, half, 1).astype(BF16)
    away, dq_got = lax.optimization_barrier((away, dq_got))
    pair = [x.reshape(resp_count, factor, tokens, width) for x in in_order(dq_own, dq_got)]
    query_grad = jnp.concatenate(pair, 1).transpose(2, 0, 1, 3)
    got = lax.ppermute(away, "tensor", [(0, 1), (1, 0)])
    prompt_input_grad = (mine + got.astype(F32)).astype(BF16)
    return (query_grad, grads[0], grads[1], prompt_input_grad)


def solution(mesh):
    placed = P("prefix", "group", "tensor", None)
    return jax.shard_map(
        per_device,
        mesh=mesh,
        in_specs=(
            placed,
            placed,
            placed,
            placed,
            P("prefix", "tensor", None),
            P("prefix", "tensor", None),
            P(None, "tensor"),
            P(None, "tensor"),
            P(),
        ),
        out_specs=(placed, placed, placed, P("prefix", "tensor")),
        check_vma=False,
    )
```

```python
import functools
import math

import jax
import jax.numpy as jnp
from jax import lax
from jax.experimental import pallas as pl
from jax.experimental.pallas import tpu as pltpu
from jax.sharding import PartitionSpec as P

MASKED = -1e30
F32 = jnp.float32
BF16 = jnp.bfloat16


def dot_nt(a, b):
    return lax.dot_general(a, b, (((1,), (1,)), ((), ())), preferred_element_type=F32)


def dot_nn(a, b):
    return lax.dot_general(a, b, (((1,), (0,)), ((), ())), preferred_element_type=F32)


def dot_tn(a, b):
    return lax.dot_general(a, b, (((0,), (0,)), ((), ())), preferred_element_type=F32)


def attention_kernel(tokens, prows, zs, count, meta, *refs):
    refs = list(refs)
    qd_hbm = [[refs.pop(0) for _ in range(2)] for _ in range(count)]
    kv_refs = [refs.pop(0) for _ in range(zs)]
    dq_hbm = [refs.pop(0) for _ in range(2)]
    dkv_hbm = [refs.pop(0) for _ in range(zs)]
    dpkv_hbm = [refs.pop(0) for _ in range(zs)]
    e_ref, dp_ref, m_ref, l_ref, a_ref, mc_ref, dqt_ref, dk_acc, dv_acc = refs[:9]
    qd_refs, dq_refs, dkv_refs, dpkv_ref, in_sem, dq_sem, dkv_sem, dpkv_sem = refs[9:]
    rows, width = qd_refs.shape[3:]

    def incoming(r, half, source=0):
        return pltpu.make_async_copy(qd_hbm[source][half], qd_refs.at[r, half], in_sem.at[r, half])

    def dq_out(r, half):
        return pltpu.make_async_copy(dq_refs.at[r, half], dq_hbm[half].at[r], dq_sem.at[r, half])

    def dkv_out(r, s):
        return pltpu.make_async_copy(dkv_refs.at[r, s], dkv_hbm[s].at[r], dkv_sem.at[r, s])

    def dpkv_out(s):
        return pltpu.make_async_copy(dpkv_ref.at[s], dpkv_hbm[s], dpkv_sem.at[s])

    for r in range(count):
        for half in range(2):
            incoming(r, half, r).start()
    scale = 1.0 / math.sqrt(width)
    log2 = scale * math.log2(math.e)
    z, xh = meta[0], meta[1]
    chunk = 2 * tokens
    pchunk = 4 * prows
    pcount = zs // 2
    pbase = 4 * tokens * count
    prompt_rows = pcount * pchunk

    def prompt_pair(c, which):
        first = pbase + which * 2 * prows
        parts = [kv_refs[2 * c + i][first : first + 2 * prows] for i in range(2)]
        return jnp.concatenate(parts, axis=0)

    def resp_pair(r, s, which):
        first = pl.multiple_of(r * (4 * tokens) + which * chunk, chunk)
        return kv_refs[s][pl.ds(first, chunk)]

    def forward(q, do, keys, values, base, index, mask):
        n = keys.shape[0]
        scores = dot_nt(keys, q)
        if mask is not None:
            scores = jnp.where(mask, scores, MASKED)
        top = jnp.max(scores, axis=0, keepdims=True)
        if index > 0:
            old = m_ref[...]
            top = jnp.maximum(old, top)
        e = jnp.exp2((scores - top) * log2)
        dp = dot_nt(values, do)
        esum = jnp.sum(e, axis=0, keepdims=True)
        dsum = jnp.sum(e * dp, axis=0, keepdims=True)
        if index > 0:
            fix = jnp.exp2((old - top) * log2)
            esum = esum + l_ref[...] * fix
            dsum = dsum + a_ref[...] * fix
        m_ref[...] = top
        l_ref[...] = esum
        a_ref[...] = dsum
        mc_ref[index] = top
        e_ref[base : base + n] = e
        dp_ref[base : base + n] = dp

    def backward(half, q, do, keys, base, index):
        n = keys.shape[0]
        inv = 1.0 / l_ref[...]
        factor = jnp.exp2((mc_ref[index] - m_ref[...]) * log2) * inv
        delta = a_ref[...] * inv
        p = e_ref[base : base + n] * factor
        ds = (p * (dp_ref[base : base + n] - delta)).astype(BF16)
        dv = dot_nn(p.astype(BF16), do)
        dk = dot_nn(ds, q)
        dqt = dot_tn(keys, ds)
        if index == 0:
            dqt_ref[...] = dqt
        else:
            dqt_ref[...] += dqt
        if half == 0 and base >= prompt_rows:
            dk_acc[base : base + n] = dk
            dv_acc[base : base + n] = dv
        else:
            dk_acc[base : base + n] += dk
            dv_acc[base : base + n] += dv

    def when_past(s, step):
        if s == 0:
            step()
        else:
            pl.when(z >= s)(step)

    def past_all(step):
        @pl.when(z == zs - 1)
        def _():
            for s in range(zs):
                step(s)

        @pl.when(z < zs - 1)
        def _():
            for s in range(zs):
                when_past(s, functools.partial(step, s))

    def one_half(r, half):
        token = lax.broadcasted_iota(jnp.int32, (rows, width), 0) & (tokens - 1)
        raw = qd_refs[r, half, 1].astype(F32)
        qd_refs[r, half, 1] = jnp.where(token < meta[2 + 2 * r + half], raw, 0.0).astype(BF16)
        q, do = qd_refs[r, half, 0], qd_refs[r, half, 1]
        for c in range(pcount):
            forward(q, do, prompt_pair(c, 0), prompt_pair(c, 1), c * pchunk, c, None)
        def forward_step(s):
            mask = None
            if s == 0:
                row = lax.broadcasted_iota(jnp.int32, (chunk, rows), 0)
                lane = lax.broadcasted_iota(jnp.int32, (1, rows), 1)
                start = (1 - xh) if half else xh
                token = (lane & (tokens - 1)) + start * tokens
                mask = (row ^ (xh * tokens)) <= token
            base = pcount * pchunk + s * chunk
            forward(q, do, resp_pair(r, s, 0), resp_pair(r, s, 1), base, pcount + s, mask)

        past_all(forward_step)
        for c in range(pcount):
            backward(half, q, do, prompt_pair(c, 0), c * pchunk, c)
        def backward_step(s):
            base = pcount * pchunk + s * chunk
            backward(half, q, do, resp_pair(r, s, 0), base, pcount + s)

        past_all(backward_step)
        dq_refs[r, half] = (dqt_ref[...] * scale).T.astype(BF16)

    dk_acc[0:prompt_rows] = jnp.zeros((prompt_rows, width), F32)
    dv_acc[0:prompt_rows] = jnp.zeros((prompt_rows, width), F32)

    @pl.loop(0, count)
    def _(r):
        for half in range(2):
            live = meta[2 + 2 * r + half]
            incoming(r, half).wait()

            @pl.when(live > 0)
            def _(half=half):
                one_half(r, half)

            @pl.when(live <= 0)
            def _(half=half):
                dq_refs[r, half] = jnp.zeros((rows, width), BF16)
                if half == 0:
                    zeros = jnp.zeros((dk_acc.shape[0] - prompt_rows, width), F32)
                    dk_acc[prompt_rows:] = zeros
                    dv_acc[prompt_rows:] = zeros

            dq_out(r, half).start()

        for s in range(zs):

            def store(s=s):
                base = prompt_rows + s * chunk
                dkv_refs[r, s, 0:chunk] = (dk_acc[base : base + chunk] * scale).astype(BF16)
                dkv_refs[r, s, chunk : 2 * chunk] = dv_acc[base : base + chunk].astype(BF16)
                dkv_out(r, s).start()

            when_past(s, store)

    for s in range(zs):
        n = 2 * prows
        span = slice(s * n, (s + 1) * n)
        dpkv_ref[s, 0:n] = (dk_acc[span] * scale).astype(BF16)
        dpkv_ref[s, n : 2 * n] = dv_acc[span].astype(BF16)
        dpkv_out(s).start()
    for s in range(zs):
        dpkv_out(s).wait()
    for r in range(count):
        for half in range(2):
            dq_out(r, half).wait()
        for s in range(zs):
            when_past(s, dkv_out(r, s).wait)


def attention(meta, qds, kvs, count, tokens, prows):
    zs = len(kvs)
    rows, width = qds[0].shape[1:]
    total = zs * 2 * (prows + tokens)
    in_vmem = pl.BlockSpec(memory_space=pltpu.VMEM)
    in_hbm = pl.BlockSpec(memory_space=pltpu.HBM)
    args = [pltpu.with_memory_space_constraint(x, pltpu.HBM) for x in qds] + list(kvs)
    in_specs = [pl.BlockSpec(memory_space=pltpu.SMEM)] + [in_hbm] * len(qds) + [in_vmem] * zs
    out_shape = [pltpu.HBM((count, rows, width), BF16)] * 2
    out_shape += [pltpu.HBM((count, 4 * tokens, width), BF16)] * zs
    out_shape += [pltpu.HBM((4 * prows, width), BF16)] * zs
    scratch = [
        pltpu.VMEM((total, rows), F32),
        pltpu.VMEM((total, rows), F32),
        pltpu.VMEM((1, rows), F32),
        pltpu.VMEM((1, rows), F32),
        pltpu.VMEM((1, rows), F32),
        pltpu.VMEM((zs // 2 + zs, 1, rows), F32),
        pltpu.VMEM((width, rows), F32),
        pltpu.VMEM((total, width), F32),
        pltpu.VMEM((total, width), F32),
        pltpu.VMEM((count, 2, 2, rows, width), BF16),
        pltpu.VMEM((count, 2, rows, width), BF16),
        pltpu.VMEM((count, zs, 4 * tokens, width), BF16),
        pltpu.VMEM((zs, 4 * prows, width), BF16),
        pltpu.SemaphoreType.DMA((count, 2)),
        pltpu.SemaphoreType.DMA((count, 2)),
        pltpu.SemaphoreType.DMA((count, zs)),
        pltpu.SemaphoreType.DMA((zs,)),
    ]
    return pl.pallas_call(
        functools.partial(attention_kernel, tokens, prows, zs, count),
        out_shape=out_shape,
        in_specs=in_specs,
        out_specs=[in_hbm] * len(out_shape),
        scratch_shapes=scratch,
        compiler_params=pltpu.CompilerParams(vmem_limit_bytes=30 * 1024 * 1024),
        cost_estimate=pl.CostEstimate(
            flops=20 * count * rows * total * width,
            bytes_accessed=8 * 1024 * 1024,
            transcendentals=2 * count * rows * total,
        ),
        name="attention_grad",
    )(meta, *args)


def per_device(
    resp_query,
    response_key,
    response_value,
    resp_cotangent,
    prompt_key,
    prompt_value_rows,
    key_matrix,
    value_matrix,
    resp_lengths,
):
    tokens, resp_count, query_heads, width = resp_query.shape
    kv_heads = response_key.shape[2]
    factor = query_heads // kv_heads
    prows = prompt_key.shape[0]
    prefix_size = lax.axis_size("prefix")
    group_size = lax.axis_size("group")
    zs = prefix_size // 2
    prefix = lax.axis_index("prefix")
    z, xh = prefix // 2, prefix % 2
    first = xh == 0

    def swap(x):
        return lax.ppermute(x, "prefix", [(i, i ^ 1) for i in range(prefix_size)])

    def shift(x, s, wrap):
        pairs = [(i, i + 2 * s) for i in range(prefix_size)]
        if wrap:
            pairs = [(i, j % prefix_size) for i, j in pairs]
        else:
            pairs = [(i, j) for i, j in pairs if 0 <= j < prefix_size]
        return lax.ppermute(x, "prefix", pairs)

    def own_away(lo, hi):
        return jnp.where(first, lo, hi), jnp.where(first, hi, lo)

    def in_order(own, other):
        return jnp.where(first, own, other), jnp.where(first, other, own)

    resp = jnp.stack((response_key, response_value), 0).transpose(3, 2, 0, 1, 4)
    prompt = jnp.stack((prompt_key, prompt_value_rows), 0).transpose(2, 0, 1, 3)
    resp_own, resp_away = own_away(resp[0], resp[1])
    prompt_own, prompt_away = own_away(prompt[0], prompt[1])
    flat = jnp.concatenate((resp_away.reshape(-1, width), prompt_away.reshape(-1, width)))
    got = swap(flat)
    split = resp_away.size // width
    resp_got = got[:split].reshape(resp_own.shape)
    prompt_got = got[split:].reshape(prompt_own.shape)
    resp_pair = jnp.stack((resp_own, resp_got), 2).reshape(resp_count, 4 * tokens, width)
    prompt_pair = jnp.stack((prompt_own, prompt_got), 1).reshape(4 * prows, width)

    own_lengths = lax.dynamic_slice_in_dim(
        resp_lengths, lax.axis_index("group") * resp_count, resp_count
    )

    message = jnp.concatenate((resp_pair.reshape(-1, width), prompt_pair))
    kvs = [message] + [shift(message, s, True) for s in range(1, zs)]

    qds = []
    for r in range(resp_count):
        pair = jnp.stack((resp_query[:, r], resp_cotangent[:, r]), 0)
        own, away = own_away(pair[:, :, :factor], pair[:, :, factor:])
        own = own.transpose(0, 2, 1, 3).reshape(2, factor * tokens, width)
        away = away.transpose(0, 2, 1, 3).reshape(2, factor * tokens, width)
        qds += [own, swap(away)]

    live = [
        own_lengths[r] - (2 * z + place) * tokens
        for r in range(resp_count)
        for place in (xh, 1 - xh)
    ]
    meta = jnp.stack([z, xh] + live).astype(jnp.int32)
    outs = list(attention(meta, qds, kvs, resp_count, tokens, prows))
    dq_own, dq_away = outs[:2]
    dkv = outs[2 : 2 + zs]
    dprompt = outs[2 + zs :]

    def exchange(x, step):
        return lax.ppermute(x, "group", [(i, i ^ step) for i in range(group_size)])

    share = dprompt[0].astype(F32)
    for s in range(1, zs):
        share = share + shift(dprompt[s], -s, True).astype(F32)
    dq_got = swap(dq_away)
    share = (share + exchange(share, 1)).astype(BF16)
    terms = [share] + [exchange(share, step) for step in range(2, group_size, 2)]
    middle = zs // 2
    terms[1], dkv[middle] = lax.optimization_barrier((terms[1], dkv[middle]))
    early = shift(dkv.pop(middle), -middle, False)
    *terms, dq_got = lax.optimization_barrier((*terms, dq_got))
    terms = [x.astype(F32) for x in terms]
    while len(terms) > 1:
        terms = [terms[i] + terms[i + 1] for i in range(0, len(terms), 2)]
    share, *dkv[1:] = lax.optimization_barrier((terms[0].astype(BF16), *dkv[1:]))
    low = share.reshape(2, 2, prows, width)
    low_got, early = lax.optimization_barrier((swap(low[:, 1]), early))
    low = jnp.concatenate(in_order(low[:, 0], low_got), 2)
    projected = dot_nt(low[0], key_matrix) + dot_nt(low[1], value_matrix)

    total = dkv[0].astype(F32) + early.astype(F32)
    for s, part in zip([s for s in range(1, zs) if s != middle], dkv[1:]):
        total = total + shift(part, -s, False).astype(F32)
    total = total.reshape(resp_count, 2, 2, tokens, width).astype(BF16)
    grads = in_order(total[:, :, 0], swap(total[:, :, 1]))
    grads = jnp.stack(grads, 2).transpose(1, 3, 0, 2, 4)

    tensor = lax.axis_index("tensor")
    half = projected.shape[1] // 2
    mine = lax.dynamic_slice_in_dim(projected, tensor * half, half, 1)
    away = lax.dynamic_slice_in_dim(projected, (1 - tensor) * half, half, 1).astype(BF16)
    away, dq_got = lax.optimization_barrier((away, dq_got))
    pair = [x.reshape(resp_count, factor, tokens, width) for x in in_order(dq_own, dq_got)]
    query_grad = jnp.concatenate(pair, 1).transpose(2, 0, 1, 3)
    got = lax.ppermute(away, "tensor", [(0, 1), (1, 0)])
    prompt_input_grad = (mine + got.astype(F32)).astype(BF16)
    return (query_grad, grads[0], grads[1], prompt_input_grad)


def solution(mesh):
    placed = P("prefix", "group", "tensor", None)
    return jax.shard_map(
        per_device,
        mesh=mesh,
        in_specs=(
            placed,
            placed,
            placed,
            placed,
            P("prefix", "tensor", None),
            P("prefix", "tensor", None),
            P(None, "tensor"),
            P(None, "tensor"),
            P(),
        ),
        out_specs=(placed, placed, placed, P("prefix", "tensor")),
        check_vma=False,
    )
```

```python
import functools
import math

import jax
import jax.numpy as jnp
from jax import lax
from jax.experimental import pallas as pl
from jax.experimental.pallas import tpu as pltpu
from jax.sharding import PartitionSpec as P

MASKED = -1e30
F32 = jnp.float32
BF16 = jnp.bfloat16


def dot_nt(a, b):
    return lax.dot_general(a, b, (((1,), (1,)), ((), ())), preferred_element_type=F32)


def dot_nn(a, b):
    return lax.dot_general(a, b, (((1,), (0,)), ((), ())), preferred_element_type=F32)


def dot_tn(a, b):
    return lax.dot_general(a, b, (((0,), (0,)), ((), ())), preferred_element_type=F32)


def attention_kernel(tokens, prows, zs, count, meta, *refs):
    refs = list(refs)
    qd_hbm = [[refs.pop(0) for _ in range(2)] for _ in range(count)]
    kv_refs = [refs.pop(0) for _ in range(zs)]
    dq_hbm = [refs.pop(0) for _ in range(2)]
    dkv_hbm = [refs.pop(0) for _ in range(zs)]
    dpkv_hbm = [refs.pop(0) for _ in range(zs)]
    e_ref, dp_ref, m_ref, l_ref, a_ref, mc_ref, dqt_ref, dk_acc, dv_acc = refs[:9]
    qd_refs, dq_refs, dkv_refs, dpkv_ref, in_sem, dq_sem, dkv_sem, dpkv_sem = refs[9:]
    rows, width = qd_refs.shape[3:]

    def incoming(r, half, source=0):
        return pltpu.make_async_copy(qd_hbm[source][half], qd_refs.at[r, half], in_sem.at[r, half])

    def dq_out(r, half):
        return pltpu.make_async_copy(dq_refs.at[r, half], dq_hbm[half].at[r], dq_sem.at[r, half])

    def dkv_out(r, s):
        return pltpu.make_async_copy(dkv_refs.at[r, s], dkv_hbm[s].at[r], dkv_sem.at[r, s])

    def dpkv_out(s):
        return pltpu.make_async_copy(dpkv_ref.at[s], dpkv_hbm[s], dpkv_sem.at[s])

    for r in range(count):
        for half in range(2):
            incoming(r, half, r).start()
    scale = 1.0 / math.sqrt(width)
    log2 = scale * math.log2(math.e)
    z, xh = meta[0], meta[1]
    chunk = 2 * tokens
    pchunk = 4 * prows
    pcount = zs // 2
    pbase = 4 * tokens * count
    prompt_rows = pcount * pchunk

    def prompt_pair(c, which):
        first = pbase + which * 2 * prows
        parts = [kv_refs[2 * c + i][first : first + 2 * prows] for i in range(2)]
        return jnp.concatenate(parts, axis=0)

    def resp_pair(r, s, which):
        first = pl.multiple_of(r * (4 * tokens) + which * chunk, chunk)
        return kv_refs[s][pl.ds(first, chunk)]

    def forward(q, do, keys, values, base, index, mask):
        n = keys.shape[0]
        scores = dot_nt(keys, q)
        if mask is not None:
            scores = jnp.where(mask, scores, MASKED)
        top = jnp.max(scores, axis=0, keepdims=True)
        if index > 0:
            old = m_ref[...]
            top = jnp.maximum(old, top)
        e = jnp.exp2((scores - top) * log2)
        dp = dot_nt(values, do)
        esum = jnp.sum(e, axis=0, keepdims=True)
        dsum = jnp.sum(e * dp, axis=0, keepdims=True)
        if index > 0:
            fix = jnp.exp2((old - top) * log2)
            esum = esum + l_ref[...] * fix
            dsum = dsum + a_ref[...] * fix
        m_ref[...] = top
        l_ref[...] = esum
        a_ref[...] = dsum
        mc_ref[index] = top
        e_ref[base : base + n] = e
        dp_ref[base : base + n] = dp

    def backward(half, q, do, keys, base, index):
        n = keys.shape[0]
        inv = 1.0 / l_ref[...]
        factor = jnp.exp2((mc_ref[index] - m_ref[...]) * log2) * inv
        delta = a_ref[...] * inv
        p = e_ref[base : base + n] * factor
        ds = (p * (dp_ref[base : base + n] - delta)).astype(BF16)
        dv = dot_nn(p.astype(BF16), do)
        dk = dot_nn(ds, q)
        dqt = dot_tn(keys, ds)
        if index == 0:
            dqt_ref[...] = dqt
        else:
            dqt_ref[...] += dqt
        if half == 0 and base >= prompt_rows:
            dk_acc[base : base + n] = dk
            dv_acc[base : base + n] = dv
        else:
            dk_acc[base : base + n] += dk
            dv_acc[base : base + n] += dv

    def when_past(s, step):
        if s == 0:
            step()
        else:
            pl.when(z >= s)(step)

    def past_all(step):
        @pl.when(z == zs - 1)
        def _():
            for s in range(zs):
                step(s)

        @pl.when(z < zs - 1)
        def _():
            for s in range(zs):
                when_past(s, functools.partial(step, s))

    def one_half(r, half):
        token = lax.broadcasted_iota(jnp.int32, (rows, width), 0) & (tokens - 1)
        raw = qd_refs[r, half, 1].astype(F32)
        qd_refs[r, half, 1] = jnp.where(token < meta[2 + 2 * r + half], raw, 0.0).astype(BF16)
        q, do = qd_refs[r, half, 0], qd_refs[r, half, 1]
        for c in range(pcount):
            forward(q, do, prompt_pair(c, 0), prompt_pair(c, 1), c * pchunk, c, None)
        def forward_step(s):
            mask = None
            if s == 0:
                row = lax.broadcasted_iota(jnp.int32, (chunk, rows), 0)
                lane = lax.broadcasted_iota(jnp.int32, (1, rows), 1)
                start = (1 - xh) if half else xh
                token = (lane & (tokens - 1)) + start * tokens
                mask = (row ^ (xh * tokens)) <= token
            base = pcount * pchunk + s * chunk
            forward(q, do, resp_pair(r, s, 0), resp_pair(r, s, 1), base, pcount + s, mask)

        past_all(forward_step)
        for c in range(pcount):
            backward(half, q, do, prompt_pair(c, 0), c * pchunk, c)
        def backward_step(s):
            base = pcount * pchunk + s * chunk
            backward(half, q, do, resp_pair(r, s, 0), base, pcount + s)

        past_all(backward_step)
        dq_refs[r, half] = (dqt_ref[...] * scale).T.astype(BF16)

    dk_acc[0:prompt_rows] = jnp.zeros((prompt_rows, width), F32)
    dv_acc[0:prompt_rows] = jnp.zeros((prompt_rows, width), F32)

    @pl.loop(0, count)
    def _(r):
        for half in range(2):
            live = meta[2 + 2 * r + half]
            incoming(r, half).wait()

            @pl.when(live > 0)
            def _(half=half):
                one_half(r, half)

            @pl.when(live <= 0)
            def _(half=half):
                dq_refs[r, half] = jnp.zeros((rows, width), BF16)
                if half == 0:
                    zeros = jnp.zeros((dk_acc.shape[0] - prompt_rows, width), F32)
                    dk_acc[prompt_rows:] = zeros
                    dv_acc[prompt_rows:] = zeros

            dq_out(r, half).start()

        for s in range(zs):

            def store(s=s):
                base = prompt_rows + s * chunk
                dkv_refs[r, s, 0:chunk] = (dk_acc[base : base + chunk] * scale).astype(BF16)
                dkv_refs[r, s, chunk : 2 * chunk] = dv_acc[base : base + chunk].astype(BF16)
                dkv_out(r, s).start()

            when_past(s, store)

    for s in range(zs):
        n = 2 * prows
        span = slice(s * n, (s + 1) * n)
        dpkv_ref[s, 0:n] = (dk_acc[span] * scale).astype(BF16)
        dpkv_ref[s, n : 2 * n] = dv_acc[span].astype(BF16)
        dpkv_out(s).start()
    for s in range(zs):
        dpkv_out(s).wait()
    for r in range(count):
        for half in range(2):
            dq_out(r, half).wait()
        for s in range(zs):
            when_past(s, dkv_out(r, s).wait)


def attention(meta, qds, kvs, count, tokens, prows):
    zs = len(kvs)
    rows, width = qds[0].shape[1:]
    total = zs * 2 * (prows + tokens)
    in_vmem = pl.BlockSpec(memory_space=pltpu.VMEM)
    in_hbm = pl.BlockSpec(memory_space=pltpu.HBM)
    args = [pltpu.with_memory_space_constraint(x, pltpu.HBM) for x in qds] + list(kvs)
    in_specs = [pl.BlockSpec(memory_space=pltpu.SMEM)] + [in_hbm] * len(qds) + [in_vmem] * zs
    out_shape = [pltpu.HBM((count, rows, width), BF16)] * 2
    out_shape += [pltpu.HBM((count, 4 * tokens, width), BF16)] * zs
    out_shape += [pltpu.HBM((4 * prows, width), BF16)] * zs
    scratch = [
        pltpu.VMEM((total, rows), F32),
        pltpu.VMEM((total, rows), F32),
        pltpu.VMEM((1, rows), F32),
        pltpu.VMEM((1, rows), F32),
        pltpu.VMEM((1, rows), F32),
        pltpu.VMEM((zs // 2 + zs, 1, rows), F32),
        pltpu.VMEM((width, rows), F32),
        pltpu.VMEM((total, width), F32),
        pltpu.VMEM((total, width), F32),
        pltpu.VMEM((count, 2, 2, rows, width), BF16),
        pltpu.VMEM((count, 2, rows, width), BF16),
        pltpu.VMEM((count, zs, 4 * tokens, width), BF16),
        pltpu.VMEM((zs, 4 * prows, width), BF16),
        pltpu.SemaphoreType.DMA((count, 2)),
        pltpu.SemaphoreType.DMA((count, 2)),
        pltpu.SemaphoreType.DMA((count, zs)),
        pltpu.SemaphoreType.DMA((zs,)),
    ]
    return pl.pallas_call(
        functools.partial(attention_kernel, tokens, prows, zs, count),
        out_shape=out_shape,
        in_specs=in_specs,
        out_specs=[in_hbm] * len(out_shape),
        scratch_shapes=scratch,
        compiler_params=pltpu.CompilerParams(vmem_limit_bytes=30 * 1024 * 1024),
        cost_estimate=pl.CostEstimate(
            flops=20 * count * rows * total * width,
            bytes_accessed=8 * 1024 * 1024,
            transcendentals=2 * count * rows * total,
        ),
        name="attention_grad",
    )(meta, *args)


def per_device(
    resp_query,
    response_key,
    response_value,
    resp_cotangent,
    prompt_key,
    prompt_value_rows,
    key_matrix,
    value_matrix,
    resp_lengths,
):
    tokens, resp_count, query_heads, width = resp_query.shape
    kv_heads = response_key.shape[2]
    factor = query_heads // kv_heads
    prows = prompt_key.shape[0]
    prefix_size = lax.axis_size("prefix")
    group_size = lax.axis_size("group")
    zs = prefix_size // 2
    prefix = lax.axis_index("prefix")
    z, xh = prefix // 2, prefix % 2
    first = xh == 0

    def swap(x):
        return lax.ppermute(x, "prefix", [(i, i ^ 1) for i in range(prefix_size)])

    def shift(x, s, wrap):
        pairs = [(i, i + 2 * s) for i in range(prefix_size)]
        if wrap:
            pairs = [(i, j % prefix_size) for i, j in pairs]
        else:
            pairs = [(i, j) for i, j in pairs if 0 <= j < prefix_size]
        return lax.ppermute(x, "prefix", pairs)

    def own_away(lo, hi):
        return jnp.where(first, lo, hi), jnp.where(first, hi, lo)

    def in_order(own, other):
        return jnp.where(first, own, other), jnp.where(first, other, own)

    resp = jnp.stack((response_key, response_value), 0).transpose(3, 2, 0, 1, 4)
    prompt = jnp.stack((prompt_key, prompt_value_rows), 0).transpose(2, 0, 1, 3)
    resp_own, resp_away = own_away(resp[0], resp[1])
    prompt_own, prompt_away = own_away(prompt[0], prompt[1])
    flat = jnp.concatenate((resp_away.reshape(-1, width), prompt_away.reshape(-1, width)))
    got = swap(flat)
    split = resp_away.size // width
    resp_got = got[:split].reshape(resp_own.shape)
    prompt_got = got[split:].reshape(prompt_own.shape)
    resp_pair = jnp.stack((resp_own, resp_got), 2).reshape(resp_count, 4 * tokens, width)
    prompt_pair = jnp.stack((prompt_own, prompt_got), 1).reshape(4 * prows, width)

    own_lengths = lax.dynamic_slice_in_dim(
        resp_lengths, lax.axis_index("group") * resp_count, resp_count
    )

    message = jnp.concatenate((resp_pair.reshape(-1, width), prompt_pair))
    kvs = [message] + [shift(message, s, True) for s in range(1, zs)]

    qds = []
    for r in range(resp_count):
        pair = jnp.stack((resp_query[:, r], resp_cotangent[:, r]), 0)
        own, away = own_away(pair[:, :, :factor], pair[:, :, factor:])
        own = own.transpose(0, 2, 1, 3).reshape(2, factor * tokens, width)
        away = away.transpose(0, 2, 1, 3).reshape(2, factor * tokens, width)
        qds += [own, swap(away)]

    live = [
        own_lengths[r] - (2 * z + place) * tokens
        for r in range(resp_count)
        for place in (xh, 1 - xh)
    ]
    meta = jnp.stack([z, xh] + live).astype(jnp.int32)
    outs = list(attention(meta, qds, kvs, resp_count, tokens, prows))
    dq_own, dq_away = outs[:2]
    dkv = outs[2 : 2 + zs]
    dprompt = outs[2 + zs :]

    def exchange(x, step):
        return lax.ppermute(x, "group", [(i, i ^ step) for i in range(group_size)])

    share = dprompt[0].astype(F32)
    for s in range(1, zs):
        share = share + shift(dprompt[s], -s, True).astype(F32)
    dq_got = swap(dq_away)
    share = (share + exchange(share, 1)).astype(BF16)
    terms = [share] + [exchange(share, step) for step in range(2, group_size, 2)]
    middle = zs // 2
    terms[1], dkv[middle] = lax.optimization_barrier((terms[1], dkv[middle]))
    early = shift(dkv.pop(middle), -middle, False)
    terms[2], dkv[-1] = lax.optimization_barrier((terms[2], dkv[-1]))
    *terms, dq_got = lax.optimization_barrier((*terms, dq_got))
    terms = [x.astype(F32) for x in terms]
    while len(terms) > 1:
        terms = [terms[i] + terms[i + 1] for i in range(0, len(terms), 2)]
    share, dkv[1] = lax.optimization_barrier((terms[0].astype(BF16), dkv[1]))
    low = share.reshape(2, 2, prows, width)
    low_got, early = lax.optimization_barrier((swap(low[:, 1]), early))
    low = jnp.concatenate(in_order(low[:, 0], low_got), 2)
    projected = dot_nt(low[0], key_matrix) + dot_nt(low[1], value_matrix)

    total = dkv[0].astype(F32) + early.astype(F32)
    for s, part in zip([s for s in range(1, zs) if s != middle], dkv[1:]):
        total = total + shift(part, -s, False).astype(F32)
    total = total.reshape(resp_count, 2, 2, tokens, width).astype(BF16)
    grads = in_order(total[:, :, 0], swap(total[:, :, 1]))
    grads = jnp.stack(grads, 2).transpose(1, 3, 0, 2, 4)

    tensor = lax.axis_index("tensor")
    half = projected.shape[1] // 2
    mine = lax.dynamic_slice_in_dim(projected, tensor * half, half, 1)
    away = lax.dynamic_slice_in_dim(projected, (1 - tensor) * half, half, 1).astype(BF16)
    away, dq_got = lax.optimization_barrier((away, dq_got))
    pair = [x.reshape(resp_count, factor, tokens, width) for x in in_order(dq_own, dq_got)]
    query_grad = jnp.concatenate(pair, 1).transpose(2, 0, 1, 3)
    got = lax.ppermute(away, "tensor", [(0, 1), (1, 0)])
    prompt_input_grad = (mine + got.astype(F32)).astype(BF16)
    return (query_grad, grads[0], grads[1], prompt_input_grad)


def solution(mesh):
    placed = P("prefix", "group", "tensor", None)
    return jax.shard_map(
        per_device,
        mesh=mesh,
        in_specs=(
            placed,
            placed,
            placed,
            placed,
            P("prefix", "tensor", None),
            P("prefix", "tensor", None),
            P(None, "tensor"),
            P(None, "tensor"),
            P(),
        ),
        out_specs=(placed, placed, placed, P("prefix", "tensor")),
        check_vma=False,
    )
```
